128 devices in a mesh: seq: 16 (over z, x), chan: 4 (over y), dp: 2 (over core).
Axes of the slice: x: 4, y: 4, z: 4, core: 2. Of those that a mesh axis runs over, the one named last changes fastest.
Arguments:
- mr_query: bfloat16 [2, 8192, 2048], P('dp', 'chan', 'seq'), may hold values from -6 to 6
- mr_key: bfloat16 [2, 8192, 2048], P('dp', 'chan', 'seq'), may hold values from -6 to 6
- mr_value: bfloat16 [2, 8192, 2048], P('dp', 'chan', 'seq'), may hold values from -6 to 6
- li_key: bfloat16 [2, 8192, 2048], P('dp', 'chan', 'seq'), may hold values from -6 to 6
- li_value: bfloat16 [2, 8192, 2048], P('dp', 'chan', 'seq'), may hold values from -6 to 6
- grad_out: bfloat16 [2, 8192, 2048], P('dp', 'chan', 'seq'), may hold values from -6 to 6
- mr_filter: bfloat16 [512, 128], P('chan'), may hold values from -0.5 to 0.5
- li_residue: float32 [512, 16], P('chan'), may hold values from -1.5 to 1.5
- li_rate: float32 [512, 16], P('chan'), may hold values from 4.8828124e-06 to 0.05
Outputs:
- grad_mr_query: bfloat16 [2, 8192, 2048], P('dp', 'chan', 'seq')
- grad_mr_key: bfloat16 [2, 8192, 2048], P('dp', 'chan', 'seq')
- grad_mr_value: bfloat16 [2, 8192, 2048], P('dp', 'chan', 'seq')
- grad_li_key: bfloat16 [2, 8192, 2048], P('dp', 'chan', 'seq')
- grad_li_value: bfloat16 [2, 8192, 2048], P('dp', 'chan', 'seq')
- grad_filter: float32 [512, 128], P('chan')
- grad_residue: float32 [512, 16], P('chan')
The draws below stay inside these ranges and needn't reach their ends.
All inputs are finite; a program needn't handle non-finite values.
Results may differ from the reference program's by a relative error of at most 0.012.
Values may be sent and summed in bfloat16 or wider, within the bound.
A program may use at most 128 MiB of HBM per device.

```python
import math
import jax
import jax.numpy as jnp
from jax import lax

CH = 8192
FILT = 128
MODES = 16
GROUPS = 512
SEQ_LEN = 2048
BATCH = 2


def levels(key, shape, shards, low, top_value):
    loudness, own = 1.0, jax.random.fold_in(key, 6)
    for axis_at, shards_of in shards:
        heights = jnp.exp(jax.random.uniform(jax.random.fold_in(own, axis_at), (shards_of,), jnp.float32, low / len(shards), top_value / len(shards)))
        loudness = loudness * jnp.repeat(heights, shape[axis_at] // shards_of).reshape([-1 if axis == axis_at else 1 for axis in range(len(shape))])
    return loudness


def normal_values(key, shape, scale, most, split=(), kind=jnp.bfloat16):
    values = scale * jax.random.normal(key, shape, jnp.float32)
    if split:
        values = values * levels(key, shape, split, -0.22, 0.18)
    return jnp.clip(values, -most, most).astype(kind)


def setup_inputs(seed: int = 0) -> dict:
    splits = jax.random.split(jax.random.key(seed), 10)
    return {
        "mr_query": normal_values(splits[0], (BATCH, CH, SEQ_LEN), 1.0, 6.0, ((0, 2), (1, 4), (2, 16))),
        "mr_key": normal_values(splits[1], (BATCH, CH, SEQ_LEN), 1.0, 6.0, ((0, 2), (1, 4), (2, 16))),
        "mr_value": normal_values(splits[2], (BATCH, CH, SEQ_LEN), 1.0, 6.0, ((0, 2), (1, 4), (2, 16))),
        "li_key": normal_values(splits[3], (BATCH, CH, SEQ_LEN), 1.0, 6.0, ((0, 2), (1, 4), (2, 16))),
        "li_value": normal_values(splits[4], (BATCH, CH, SEQ_LEN), 1.0, 6.0, ((0, 2), (1, 4), (2, 16))),
        "grad_out": normal_values(splits[5], (BATCH, CH, SEQ_LEN), 1.0, 6.0, ((0, 2), (1, 4), (2, 16))),
        "mr_filter": normal_values(splits[6], (GROUPS, FILT), FILT ** -0.5, 0.5, ((0, 4),)),
        "li_residue": normal_values(splits[7], (GROUPS, MODES), MODES ** -0.5, 1.5, ((0, 4),), jnp.float32),
        "li_rate": jnp.clip(jnp.exp(math.log(0.05) - 9.2340569 * jax.random.uniform(splits[8], (GROUPS, MODES), jnp.float32) ** levels(splits[8], (GROUPS, MODES), ((0, 4),), -0.2, 0.2)), 4.882812390860636e-06, 0.05),
    }


exact_mode = lax.Precision.HIGHEST

def circulant_ref(entries):
    extent = entries.shape[-1]
    index = (jnp.arange(extent)[:, None] - jnp.arange(extent)[None, :]) % extent
    return entries[..., index]

def diagonal_ref(matrix):
    extent = matrix.shape[-1]
    index = (jnp.arange(extent)[:, None] - jnp.arange(extent)[None, :]) % extent
    picked = jnp.take_along_axis(matrix, jnp.broadcast_to(index, matrix.shape), axis=-1)
    return lax.optimization_barrier(jnp.sum(picked, axis=-2))

def sequence_grads(mr_query, mr_key, mr_value, li_key, li_value, grad_out, mr_filter, li_residue, li_rate):
    groups, filt_len = mr_filter.shape
    channels = mr_query.shape[0]
    group_size = channels // groups
    tile_count = mr_query.shape[1] // filt_len
    mode_count = li_rate.shape[1]
    shape_tiles = (groups, group_size, tile_count, filt_len)
    query_f = mr_query.reshape(shape_tiles).astype(jnp.float32)
    key_f = mr_key.reshape(shape_tiles).astype(jnp.float32)
    value_f = mr_value.reshape(shape_tiles).astype(jnp.float32)
    key_two = li_key.reshape(shape_tiles).astype(jnp.float32)
    value_two = li_value.reshape(shape_tiles).astype(jnp.float32)
    grad_f = grad_out.reshape(shape_tiles).astype(jnp.float32)
    lower_mask = jnp.arange(filt_len)[:, None] >= jnp.arange(filt_len)[None, :]
    circ = circulant_ref(mr_filter).astype(jnp.float32)
    toeplitz_now = jnp.where(lower_mask, circ, jnp.float32(0.0))
    toeplitz_prev = jnp.where(lower_mask, jnp.float32(0.0), circ)
    product_one = (mr_query * mr_key).reshape(shape_tiles).astype(jnp.float32)
    zero_tile = jnp.zeros_like(product_one[:, :, :1])
    product_prev = jnp.concatenate([zero_tile, product_one[:, :, :-1]], 2)
    conv_one = jnp.einsum('gcnb,gab->gcna', product_one, toeplitz_now, precision=exact_mode) + jnp.einsum('gcnb,gab->gcna', product_prev, toeplitz_prev, precision=exact_mode)
    output_one = (value_f * conv_one).astype(jnp.bfloat16)
    output_f = output_one.astype(jnp.float32)
    input_two = output_f * key_two
    offsets = jnp.arange(filt_len).astype(jnp.float32)
    gains = jnp.sqrt(-jnp.expm1(-2.0 * li_rate))
    coeffs = li_residue * gains
    powers = jnp.exp(-li_rate[:, :, None] * offsets)
    to_end = jnp.exp(-li_rate[:, :, None] * (filt_len - 1 - offsets))
    after_one = jnp.exp(-li_rate[:, :, None] * (offsets + 1))
    to_next = jnp.exp(-li_rate[:, :, None] * (filt_len - offsets))
    tile_decay = jnp.exp(-li_rate * filt_len)[:, None, :]
    local_filter = jnp.einsum('gm,gmk->gk', coeffs, powers, precision=exact_mode)
    toeplitz_li = jnp.where(lower_mask, circulant_ref(local_filter), jnp.float32(0.0))
    conv_intra = jnp.einsum('gcnb,gab->gcna', input_two, toeplitz_li, precision=exact_mode)
    tile_sums = jnp.einsum('gcnb,gmb->ngcm', input_two, to_end, precision=exact_mode)

    def forward(state, piece):
        return (tile_decay * state + piece, state)
    start = jnp.zeros((groups, group_size, mode_count), jnp.float32)
    _, state_before = lax.scan(forward, start, tile_sums)
    conv_cross = jnp.einsum('ngcm,gma->gcna', state_before, coeffs[:, :, None] * after_one, precision=exact_mode)
    conv_two = conv_intra + conv_cross
    grad_value_two = (grad_f * conv_two).astype(jnp.bfloat16)
    grad_conv_two = grad_f * value_two
    back_sums = jnp.einsum('gcna,gma->ngcm', grad_conv_two, powers, precision=exact_mode)

    def backward(state, piece):
        return (piece + tile_decay * state, state)
    _, state_after = lax.scan(backward, start, back_sums, reverse=True)
    grad_input_two = jnp.einsum('gcna,gab->gcnb', grad_conv_two, toeplitz_li, precision=exact_mode) + jnp.einsum('ngcm,gmb->gcnb', state_after, coeffs[:, :, None] * to_next, precision=exact_mode)
    grad_key_two = (grad_input_two * output_f).astype(jnp.bfloat16)
    grad_mid = grad_input_two * key_two
    energy = jnp.einsum('gcna,gcnb->gab', grad_conv_two, input_two, precision=exact_mode)
    lag_sums = diagonal_ref(jnp.where(lower_mask, energy, jnp.float32(0.0)))
    intra_term = jnp.einsum('gk,gmk->gm', lag_sums, powers, precision=exact_mode)
    cross_weight = jnp.einsum('gcna,gma->ngcm', grad_conv_two, after_one, precision=exact_mode)
    cross_term = lax.optimization_barrier(jnp.sum(state_before * cross_weight, axis=(0, 2)))
    residue_part = gains * (intra_term + cross_term)
    grad_conv_one = (grad_mid * value_f).astype(jnp.bfloat16).astype(jnp.float32)
    grad_value_one = (grad_mid * conv_one).astype(jnp.bfloat16)
    grad_next = jnp.concatenate([grad_conv_one[:, :, 1:], zero_tile], 2)
    grad_product = jnp.einsum('gcna,gab->gcnb', grad_conv_one, toeplitz_now, precision=exact_mode) + jnp.einsum('gcna,gab->gcnb', grad_next, toeplitz_prev, precision=exact_mode)
    grad_query = (grad_product * key_f).astype(jnp.bfloat16)
    grad_key = (grad_product * query_f).astype(jnp.bfloat16)
    lag_now = jnp.einsum('gcna,gcnb->gab', grad_conv_one, product_one, precision=exact_mode)
    lag_prev = jnp.einsum('gcna,gcnb->gab', grad_conv_one, product_prev, precision=exact_mode)
    filter_part = diagonal_ref(jnp.where(lower_mask, lag_now, lag_prev))
    flat_shape = mr_query.shape
    return (grad_query.reshape(flat_shape), grad_key.reshape(flat_shape), grad_value_one.reshape(flat_shape), grad_key_two.reshape(flat_shape), grad_value_two.reshape(flat_shape), filter_part, residue_part)

def reference(mr_query, mr_key, mr_value, li_key, li_value, grad_out, mr_filter, li_residue, li_rate):

    def one_sequence(streams):
        return sequence_grads(streams[0], streams[1], streams[2], streams[3], streams[4], streams[5], mr_filter, li_residue, li_rate)
    results = lax.map(one_sequence, (mr_query, mr_key, mr_value, li_key, li_value, grad_out))
    return (results[0], results[1], results[2], results[3], results[4], lax.optimization_barrier(jnp.sum(results[5], axis=0)), lax.optimization_barrier(jnp.sum(results[6], axis=0)))
```

```python
import functools

import jax
import jax.numpy as jnp
from jax import lax
from jax.experimental import pallas as pl
from jax.experimental.pallas import tpu as pltpu
from jax.sharding import PartitionSpec as P

MESH = pl.DeviceIdType.MESH
NN = (((1,), (0,)), ((), ()))
NT = (((1,), (1,)), ((), ()))
EXACT = lax.Precision.HIGHEST
BF = jnp.bfloat16
F32 = jnp.float32

L = 128
C = 16
G = 8
X = 4
CHUNKS = 2


def dot(a, b, dims):
    return lax.dot_general(a, b, dims, preferred_element_type=F32)


def dot_exact(a, b, dims):
    return lax.dot_general(a, b, dims, precision=EXACT, preferred_element_type=F32)


def one_minus_exp_neg(x):
    acc = jnp.full_like(x, 1.0 / 40320.0)
    for divisor in (5040.0, 720.0, 120.0, 24.0, 6.0, 2.0, 1.0):
        acc = 1.0 / divisor - x * acc
    return x * acc


def kernel(
    nseq, q_h, k_h, v_h, lk_h, lv_h, go_h, filt, resid, rate,
    gq_h, gk_h, gv_h, glk_h, glv_h, gf_o, gr_o,
    q, k, v, lk, lv, go, gq, gk, gv, glk, glv,
    u1, u1p, dz2, dz1, dz1n, u2, du2, z2i,
    tp, tq, hs, tn, tv,
    r_s, coef_s, gain_s, s_loc, b_in, pref_b, pref_s,
    row_b, row_s, z_b, z_s, part, rs, dpx, total,
    in_sem, out_sem, halo_ss, halo_rs, halo2_ss, halo2_rs,
    xb_ss, xb_rs, zb_ss, zb_rs, xs_ss, xs_rs, zs_ss, zs_rs,
    rs_ss, rs_rs, dp_ss, dp_rs, ag_ss, ag_rs,
):
    channels = q.shape[0]
    nb = channels // L
    per = nb // CHUNKS
    Z = nseq // X
    me = lax.axis_index("seq")
    dp = lax.axis_index("dp")
    z = me // X
    x = me - z * X

    ins = ((q_h, q), (k_h, k), (go_h, go), (lv_h, lv), (lk_h, lk), (v_h, v))
    loads = [pltpu.make_async_copy(s, d, in_sem.at[i]) for i, (s, d) in enumerate(ins)]
    for load in loads:
        load.start()

    barrier = pltpu.get_barrier_semaphore()
    for d in range(1, nseq):
        pl.semaphore_signal(
            barrier, inc=1, device_id={"seq": lax.rem(me + d, nseq)}, device_id_type=MESH
        )
    pl.semaphore_signal(barrier, inc=1, device_id={"dp": 1 - dp}, device_id_type=MESH)

    def remote(src, dst, ss, rsem, **where):
        return pltpu.make_async_remote_copy(
            src_ref=src, dst_ref=dst, send_sem=ss, recv_sem=rsem,
            device_id=where, device_id_type=MESH,
        )

    sub = lax.broadcasted_iota(jnp.int32, (L, L), 0)
    lane = lax.broadcasted_iota(jnp.int32, (L, L), 1)
    sub_f = sub.astype(F32)
    same = (sub // C) == (lane // C)
    lower = lane >= sub
    rev = (sub + lane == L - 1).astype(F32).astype(BF)
    keep = sub + lane <= L - 1
    pick8 = lax.broadcasted_iota(jnp.int32, (G, L), 1) // C == lax.broadcasted_iota(
        jnp.int32, (G, L), 0
    )
    lane_group = lax.broadcasted_iota(jnp.int32, (1, L), 1) // C
    group_mask = [(lane_group == g).astype(F32).astype(BF) for g in range(G)]

    sel = (
        lax.broadcasted_iota(jnp.int32, (C, L), 1) % C
        == lax.broadcasted_iota(jnp.int32, (C, L), 0)
    ).astype(F32)
    spread = ((sub % G) == (lane // C))

    def to_rows(mat):
        wide = dot_exact(mat, sel, NN)
        return jnp.where(spread, wide, 0.0).reshape(nb, G, L).sum(axis=1)

    r_rows = to_rows(rate[...])
    gain_rows = jnp.sqrt(one_minus_exp_neg(2.0 * r_rows))
    r_s[...] = r_rows
    gain_s[...] = gain_rows
    coef_s[...] = to_rows(resid[...]) * gain_rows

    def rows(b):
        return pl.ds(pl.multiple_of(b * L, L), L)

    def tile(b):
        return pl.ds(pl.multiple_of(b * C, C), C)

    def blocks(ch, body):
        def step(i, carry):
            body(ch * per + i)
            return carry

        lax.fori_loop(0, per, step, 0)

    def big_rows(ch):
        return pl.ds(ch * per * L, per * L)

    def small_rows(ch):
        return pl.ds(ch * per * C, per * C)

    def f(ref, idx):
        return ref[idx, :].astype(F32)

    def squeeze_modes(full):
        return jnp.where(same, full, 0.0).reshape(G, C, L).sum(axis=0)

    def widen_modes(t):
        return jnp.where(same, jnp.concatenate([t] * G, axis=0), 0.0).astype(BF)

    def phase_a(ch):
        def body(b):
            u1[rows(b), :] = (f(q, rows(b)) * f(k, rows(b))).astype(BF)

        blocks(ch, body)

    def halo(ch):
        part_rows = big_rows(ch)
        return remote(
            u1.at[part_rows], u1p.at[part_rows], halo_ss.at[ch], halo_rs.at[ch],
            seq=lax.rem(me + 1, nseq),
        )

    def halo_back(ch):
        part_rows = big_rows(ch)
        return remote(
            dz1.at[part_rows], dz1n.at[part_rows], halo2_ss.at[ch], halo2_rs.at[ch],
            seq=lax.rem(me + nseq - 1, nseq),
        )

    def row_copy(ref, ss, rsem, ch, d):
        return remote(
            ref.at[x, small_rows(ch)], ref.at[x, small_rows(ch)], ss.at[ch, d], rsem.at[ch, d],
            seq=z * X + lax.rem(x + d, X),
        )

    def z_copy(ref, ss, rsem, ch, d, sign):
        to = lax.rem(z + sign * d + Z, Z)
        return remote(
            ref.at[z, small_rows(ch)], ref.at[z, small_rows(ch)], ss.at[ch, d], rsem.at[ch, d],
            seq=to * X + x,
        )

    def phase_b(ch):
        def body(b):
            d2 = (f(go, rows(b)) * f(lv, rows(b))).astype(BF)
            dz2[rows(b), :] = d2
            r = r_s[pl.ds(b, 1), :]
            powers = jnp.exp(-r * sub_f).astype(BF)
            tp[b] = powers
            tq[b] = jnp.exp(-r * (L - 1.0 - sub_f)).astype(BF)
            row_b[x, tile(b), :] = squeeze_modes(dot(d2, powers, NN)).astype(BF)

        blocks(ch, body)

    def phase_h(ch):
        def body(b):
            r = r_s[pl.ds(b, 1), :]
            powers = jnp.exp(-r * sub_f)
            amp = jnp.where(pick8, jnp.broadcast_to(coef_s[pl.ds(b, 1), :], (G, L)), 0.0)
            h = dot_exact(amp, powers, NT)
            d2 = dz2[rows(b), :]
            outs = []
            for g in range(G):
                circ = pltpu.roll(
                    jnp.broadcast_to(h[g : g + 1], (L, L)), 0, 1, stride=1, stride_axis=0
                )
                mat = jnp.where(lower, circ, 0.0).astype(BF)
                hs[b * G + g] = mat
                outs.append(dot(d2[g * C : (g + 1) * C], mat, NT))
            du2[rows(b), :] = jnp.concatenate(outs, axis=0)

        blocks(ch, body)

    def phase_t(ch):
        def body(b):
            fl = filt[pl.ds(pl.multiple_of(b * G, G), G), :]
            for g in range(G):
                circ = pltpu.roll(
                    jnp.broadcast_to(fl[g : g + 1], (L, L)), 0, 1, stride=1, stride_axis=0
                )
                tn[b * G + g] = jnp.where(lower, circ, 0.0).astype(BF)
                tv[b * G + g] = jnp.where(lower, 0.0, circ).astype(BF)

        blocks(ch, body)

    def decay(r, steps, ok):
        return jnp.where(ok, jnp.exp(-r * (L * jnp.maximum(steps, 0)).astype(F32)), 0.0)

    def mid(ch, row, pref, zref, back):
        def body(b):
            r = r_s[pl.ds(b, 1), :]
            before = jnp.zeros((C, L), F32)
            whole = jnp.zeros((C, L), F32)
            for src in range(X):
                val = row[src, tile(b), :].astype(F32)
                gap = (src - x - 1) if back else (x - 1 - src)
                before = before + decay(r, gap, gap >= 0) * val
                whole = whole + jnp.exp(-r * float(L * (src if back else X - 1 - src))) * val
            pref[tile(b), :] = before
            zref[z, tile(b), :] = whole.astype(BF)

        blocks(ch, body)

    def incoming(b, pref, zref, back):
        r = r_s[pl.ds(b, 1), :]
        acc = jnp.zeros((C, L), F32)
        for src in range(Z):
            gap = (src - z - 1) if back else (z - 1 - src)
            val = zref[src, tile(b), :].astype(F32)
            acc = acc + jnp.where(gap >= 0, decay(r, gap * X, gap >= 0) * val, 0.0)
        steps = (X - 1 - x) if back else x
        return pref[tile(b), :] + decay(r, steps, steps >= 0) * acc

    def scaled(b, state):
        r = r_s[pl.ds(b, 1), :]
        return widen_modes(coef_s[pl.ds(b, 1), :] * jnp.exp(-r) * state)

    def phase_bz(ch):
        def body(b):
            state = incoming(b, pref_b, z_b, True)
            b_in[tile(b), :] = state
            full = du2[rows(b), :] + dot(scaled(b, state), tq[b], NT)
            du2[rows(b), :] = full
            dz1[rows(b), :] = (full * f(lk, rows(b)) * f(v, rows(b))).astype(BF)

        blocks(ch, body)

    def phase_u(ch):
        def body(b):
            now, prev = u1[rows(b), :], u1p[rows(b), :]
            outs = []
            for g in range(G):
                part_g = slice(g * C, (g + 1) * C)
                outs.append(
                    dot(now[part_g], tn[b * G + g], NN) + dot(prev[part_g], tv[b * G + g], NN)
                )
            z1 = jnp.concatenate(outs, axis=0)
            y1 = (f(v, rows(b)) * z1).astype(BF).astype(F32)
            full = du2[rows(b), :]
            key = f(lk, rows(b))
            glk[rows(b), :] = (full * y1).astype(BF)
            gv[rows(b), :] = (full * key * z1).astype(BF)
            second = (y1 * key).astype(BF)
            u2[rows(b), :] = second
            state = squeeze_modes(dot(second, tq[b], NN))
            s_loc[tile(b), :] = state
            row_s[x, tile(b), :] = state.astype(BF)

        blocks(ch, body)

    def fold(mat):
        return pltpu.roll(mat, 1, 1, stride=1, stride_axis=0).sum(axis=0, keepdims=True)

    unfold = ((sub + lane) % L == 0).astype(F32)

    def phase_e(ch):
        def body(b):
            second = u2[rows(b), :]
            flip1 = dot(rev, dz1[rows(b), :], NT).astype(BF)
            flip2 = dot(rev, dz2[rows(b), :], NT).astype(BF)
            wide = jnp.concatenate([u1p[rows(b), :], u1[rows(b), :]], axis=1)
            lag1, lag2, outs = [], [], []
            for g in range(G):
                e1 = dot(flip1 * group_mask[g], wide, NN)
                lag1.append(fold(jnp.where(keep, e1[:, L:], e1[:, :L])))
                e2 = dot(flip2 * group_mask[g], second, NN)
                lag2.append(fold(jnp.where(keep, e2, 0.0)))
                outs.append(dot(second[g * C : (g + 1) * C], hs[b * G + g], NN))
            z2i[rows(b), :] = jnp.concatenate(outs, axis=0)
            filt_sum = dot_exact(jnp.concatenate(lag1, axis=0), unfold, NN)
            r = r_s[pl.ds(b, 1), :]
            table = jnp.exp(-r * ((L - sub) % L).astype(F32))
            inner = dot_exact(jnp.concatenate(lag2, axis=0), table, NN)
            inner = jnp.where(pick8, inner, 0.0).sum(axis=0, keepdims=True)
            cross = (s_loc[tile(b), :] * b_in[tile(b), :]).sum(axis=0, keepdims=True)
            res = gain_s[pl.ds(b, 1), :] * (inner + jnp.exp(-r) * cross)
            part[b, 0:G, :] = filt_sum
            part[b, G : 2 * G, :] = jnp.broadcast_to(res, (G, L))

        blocks(ch, body)

    def phase_sz(ch):
        def body(b):
            state = incoming(b, pref_s, z_s, False)
            full = z2i[rows(b), :] + dot(scaled(b, state), tp[b], NT)
            glv[rows(b), :] = (f(go, rows(b)) * full).astype(BF)

        blocks(ch, body)

    def phase_d(ch):
        def body(b):
            now, after = dz1[rows(b), :], dz1n[rows(b), :]
            outs = []
            for g in range(G):
                part_g = slice(g * C, (g + 1) * C)
                outs.append(
                    dot(now[part_g], tn[b * G + g], NT) + dot(after[part_g], tv[b * G + g], NT)
                )
            du1 = jnp.concatenate(outs, axis=0)
            gq[rows(b), :] = (du1 * f(k, rows(b))).astype(BF)
            gk[rows(b), :] = (du1 * f(q, rows(b))).astype(BF)

        blocks(ch, body)

    def start_row(ref, ss, rsem, ch):
        for d in range(1, X):
            row_copy(ref, ss, rsem, ch, d).start()

    def wait_row(ref, ss, rsem, ch):
        for d in range(1, X):
            row_copy(ref, ss, rsem, ch, d).wait_recv()

    def z_there(d, sign):
        return (z + d < Z) if sign > 0 else (z - d >= 0)

    def z_from(d, sign):
        return (z - d >= 0) if sign > 0 else (z + d < Z)

    def start_z(ref, ss, rsem, ch, sign):
        for d in range(1, Z):
            @pl.when(z_there(d, sign))
            def _():
                z_copy(ref, ss, rsem, ch, d, sign).start()

    def wait_z(ref, ss, rsem, ch, sign):
        for d in range(1, Z):
            @pl.when(z_from(d, sign))
            def _():
                z_copy(ref, ss, rsem, ch, d, sign).wait_recv()

    results = ((gq, gq_h), (gk, gk_h), (gv, gv_h), (glk, glk_h), (glv, glv_h))

    def save(i, ch):
        src, dst = results[i]
        part_rows = big_rows(ch)
        return pltpu.make_async_copy(src.at[part_rows], dst.at[part_rows], out_sem.at[i, ch])

    every = range(CHUNKS)

    @pl.when(me == 0)
    def _():
        u1p[...] = jnp.zeros_like(u1p)

    @pl.when(me == nseq - 1)
    def _():
        dz1n[...] = jnp.zeros_like(dz1n)

    loads[0].wait()
    loads[1].wait()
    for ch in every:
        phase_a(ch)
    pl.semaphore_wait(barrier, nseq)
    for ch in every:
        @pl.when(me < nseq - 1)
        def _():
            halo(ch).start()
    loads[2].wait()
    loads[3].wait()
    for ch in every:
        phase_b(ch)
        start_row(row_b, xb_ss, xb_rs, ch)
    for ch in every:
        phase_h(ch)
    for ch in every:
        wait_row(row_b, xb_ss, xb_rs, ch)
        mid(ch, row_b, pref_b, z_b, True)
        start_z(z_b, zb_ss, zb_rs, ch, -1)
    for ch in every:
        phase_t(ch)
    loads[4].wait()
    loads[5].wait()
    for ch in every:
        wait_z(z_b, zb_ss, zb_rs, ch, -1)
        phase_bz(ch)
        @pl.when(me > 0)
        def _():
            halo_back(ch).start()
    for ch in every:
        @pl.when(me > 0)
        def _():
            halo(ch).wait_recv()
        phase_u(ch)
        start_row(row_s, xs_ss, xs_rs, ch)
        save(2, ch).start()
        save(3, ch).start()
    for ch in every:
        phase_e(ch)
    for d in range(1, nseq):
        to = lax.rem(me + d, nseq)
        remote(part.at[to], rs.at[me], rs_ss.at[d], rs_rs.at[d], seq=to).start()
    for ch in every:
        wait_row(row_s, xs_ss, xs_rs, ch)
        mid(ch, row_s, pref_s, z_s, False)
        start_z(z_s, zs_ss, zs_rs, ch, 1)
    rs[me] = part[me]
    for d in range(1, nseq):
        to = lax.rem(me + d, nseq)
        remote(part.at[to], rs.at[me], rs_ss.at[d], rs_rs.at[d], seq=to).wait_recv()
    own = rs[0]
    for i in range(1, nseq):
        own = own + rs[i]
    dpx[0] = own
    swap = remote(dpx.at[0], dpx.at[1], dp_ss, dp_rs, dp=1 - dp)
    swap.start()
    for ch in every:
        wait_z(z_s, zs_ss, zs_rs, ch, 1)
        phase_sz(ch)
        save(4, ch).start()
    swap.wait_recv()
    total[me] = dpx[0] + dpx[1]
    for d in range(1, nseq):
        to = lax.rem(me + d, nseq)
        remote(total.at[me], total.at[me], ag_ss.at[d], ag_rs.at[d], seq=to).start()
    for ch in every:
        @pl.when(me < nseq - 1)
        def _():
            halo_back(ch).wait_recv()
        phase_d(ch)
        save(0, ch).start()
        save(1, ch).start()
    for d in range(1, nseq):
        to = lax.rem(me + d, nseq)
        remote(total.at[me], total.at[me], ag_ss.at[d], ag_rs.at[d], seq=to).wait_recv()
    final = total[...]
    gf_o[...] = final[:, :G, :].reshape(nb * G, L)
    gr_o[...] = dot_exact(
        jnp.where(spread, final[:, G:, :].reshape(nb * G, L), 0.0), sel, NT
    )

    for ch in every:
        @pl.when(me < nseq - 1)
        def _():
            halo(ch).wait_send()

        @pl.when(me > 0)
        def _():
            halo_back(ch).wait_send()

        for d in range(1, X):
            row_copy(row_b, xb_ss, xb_rs, ch, d).wait_send()
            row_copy(row_s, xs_ss, xs_rs, ch, d).wait_send()
        for d in range(1, Z):
            @pl.when(z_there(d, -1))
            def _():
                z_copy(z_b, zb_ss, zb_rs, ch, d, -1).wait_send()

            @pl.when(z_there(d, 1))
            def _():
                z_copy(z_s, zs_ss, zs_rs, ch, d, 1).wait_send()

        for i in range(5):
            save(i, ch).wait()
    swap.wait_send()
    for d in range(1, nseq):
        to = lax.rem(me + d, nseq)
        remote(part.at[to], rs.at[me], rs_ss.at[d], rs_rs.at[d], seq=to).wait_send()
        remote(total.at[me], total.at[me], ag_ss.at[d], ag_rs.at[d], seq=to).wait_send()


def per_device(nseq, q, k, v, lk, lv, go, filt, resid, rate):
    channels = q.shape[1]
    groups = filt.shape[0]
    nb = channels // L
    Z = nseq // X
    big = jax.ShapeDtypeStruct((channels, L), BF)
    hbm = pl.BlockSpec(memory_space=pl.ANY)
    vmem = pl.BlockSpec(memory_space=pltpu.VMEM)
    dma = pltpu.SemaphoreType.DMA
    bigs = [pltpu.VMEM((channels, L), BF)]
    outs = pl.pallas_call(
        functools.partial(kernel, nseq),
        out_shape=[big] * 5
        + [jax.ShapeDtypeStruct((groups, L), F32), jax.ShapeDtypeStruct((groups, C), F32)],
        in_specs=[hbm] * 6 + [vmem] * 3,
        out_specs=[hbm] * 5 + [vmem] * 2,
        scratch_shapes=bigs * 11
        + bigs * 6
        + [pltpu.VMEM((channels, L), F32)] * 2
        + [pltpu.VMEM((nb, L, L), BF)] * 2
        + [pltpu.VMEM((groups, L, L), BF)] * 3
        + [pltpu.VMEM((nb, L), F32)] * 3
        + [pltpu.VMEM((nb * C, L), F32)] * 4
        + [pltpu.VMEM((X, nb * C, L), BF)] * 2
        + [pltpu.VMEM((Z, nb * C, L), BF)] * 2
        + [pltpu.VMEM((nseq, 2 * G, L), F32)] * 2
        + [pltpu.VMEM((2, 2 * G, L), F32), pltpu.VMEM((nseq, 2 * G, L), F32)]
        + [dma((6,)), dma((5, CHUNKS))]
        + [dma((CHUNKS,))] * 4
        + [dma((CHUNKS, X))] * 2
        + [dma((CHUNKS, Z))] * 2
        + [dma((CHUNKS, X))] * 2
        + [dma((CHUNKS, Z))] * 2
        + [dma((nseq,))] * 2
        + [dma, dma]
        + [dma((nseq,))] * 2,
        compiler_params=pltpu.CompilerParams(
            collective_id=0, has_side_effects=True, vmem_limit_bytes=52 * 1024 * 1024
        ),
        name="hyena_bwd",
    )(
        q[0], k[0], v[0], lk[0], lv[0], go[0], filt.astype(F32), resid, rate
    )
    return tuple(o[None] for o in outs[:5]) + tuple(outs[5:])


def solution(mesh):
    wide = P("dp", "chan", "seq")
    small = P("chan", None)
    return jax.shard_map(
        functools.partial(per_device, mesh.shape["seq"]),
        mesh=mesh,
        in_specs=(wide,) * 6 + (small,) * 3,
        out_specs=(wide,) * 5 + (small,) * 2,
        check_vma=False,
    )
```

```python
import functools

import jax
import jax.numpy as jnp
from jax import lax
from jax.experimental import pallas as pl
from jax.experimental.pallas import tpu as pltpu
from jax.sharding import PartitionSpec as P

MESH = pl.DeviceIdType.MESH
NN = (((1,), (0,)), ((), ()))
NT = (((1,), (1,)), ((), ()))
TN = (((0,), (0,)), ((), ()))
EXACT = lax.Precision.HIGHEST
BF = jnp.bfloat16
F32 = jnp.float32

L = 128
C = 16
G = 8
X = 4
CHUNKS = 2
BATCH = 4
WEIGHTS = 29


def dot(a, b, dims):
    return lax.dot_general(a, b, dims, preferred_element_type=F32)


def dot_exact(a, b, dims):
    return lax.dot_general(a, b, dims, precision=EXACT, preferred_element_type=F32)


def one_minus_exp_neg(x):
    acc = jnp.full_like(x, 1.0 / 40320.0)
    for divisor in (5040.0, 720.0, 120.0, 24.0, 6.0, 2.0, 1.0):
        acc = 1.0 / divisor - x * acc
    return x * acc


def kernel(
    nseq, q_h, k_h, v_h, lk_h, lv_h, go_h, filt, resid, rate,
    gq_h, gk_h, gv_h, glk_h, glv_h, gf_o, gr_o,
    q, k, v, lk, lv, go, gq, gk, gv, glk, glv,
    u1, u1p, dz2, dz1, dz1n, u2, du2, z2i,
    tp, tq, hs, tw, h_s, f_s, lag1, lag2,
    r_s, coef_s, gain_s, wt, s_loc, b_in, pref_b, pref_s,
    row_b, row_s, z_b, z_s, part, rs, dpx, total,
    in_sem, out_sem, halo_ss, halo_rs, halo2_ss, halo2_rs,
    xb_ss, xb_rs, zb_ss, zb_rs, xs_ss, xs_rs, zs_ss, zs_rs,
    rs_ss, rs_rs, dp_ss, dp_rs, ag_ss, ag_rs,
):
    channels = q.shape[0]
    nb = channels // L
    per = nb // CHUNKS
    Z = nseq // X
    me = lax.axis_index("seq")
    dp = lax.axis_index("dp")
    z = me // X
    x = me - z * X

    ins = ((q_h, q), (k_h, k), (go_h, go), (lv_h, lv), (lk_h, lk), (v_h, v))
    loads = [pltpu.make_async_copy(s, d, in_sem.at[i]) for i, (s, d) in enumerate(ins)]
    for load in loads:
        load.start()

    barrier = pltpu.get_barrier_semaphore()
    for d in range(1, nseq):
        pl.semaphore_signal(
            barrier, inc=1, device_id={"seq": lax.rem(me + d, nseq)}, device_id_type=MESH
        )
    pl.semaphore_signal(barrier, inc=1, device_id={"dp": 1 - dp}, device_id_type=MESH)

    def remote(src, dst, ss, rsem, **where):
        return pltpu.make_async_remote_copy(
            src_ref=src, dst_ref=dst, send_sem=ss, recv_sem=rsem,
            device_id=where, device_id_type=MESH,
        )

    sub = lax.broadcasted_iota(jnp.int32, (L, L), 0)
    lane = lax.broadcasted_iota(jnp.int32, (L, L), 1)
    sub_f = sub.astype(F32)
    same = (sub // C) == (lane // C)
    lower = lane >= sub
    rev = (sub + lane == L - 1).astype(F32).astype(BF)
    keep = sub + lane <= L - 1
    pick8 = lax.broadcasted_iota(jnp.int32, (G, L), 1) // C == lax.broadcasted_iota(
        jnp.int32, (G, L), 0
    )
    lane_group = lax.broadcasted_iota(jnp.int32, (1, L), 1) // C
    group_mask = [(lane_group == g).astype(F32).astype(BF) for g in range(G)]

    sel = (
        lax.broadcasted_iota(jnp.int32, (C, L), 1) % C
        == lax.broadcasted_iota(jnp.int32, (C, L), 0)
    ).astype(F32)
    spread = ((sub % G) == (lane // C))

    def to_rows(mat):
        wide = dot_exact(mat, sel, TN)
        return jnp.where(spread, wide, 0.0).reshape(nb, G, L).sum(axis=1)

    r_rows = to_rows(rate[...])
    gain_rows = jnp.sqrt(one_minus_exp_neg(2.0 * r_rows))
    r_s[...] = r_rows
    gain_s[...] = gain_rows
    coef_rows = to_rows(resid[...]) * gain_rows
    coef_s[...] = coef_rows
    f_s[...] = filt[...].astype(F32)

    def decay(steps):
        if isinstance(steps, int):
            return jnp.exp(-r_rows * float(L * steps))
        ok = steps >= 0
        return jnp.where(ok, jnp.exp(-r_rows * (L * jnp.maximum(steps, 0)).astype(F32)), 0.0)

    for back in (0, 1):
        base = back * 13
        for i in range(X):
            wt[base + i] = decay((i - x - 1) if back else (x - 1 - i))
            wt[base + 4 + i] = decay(i if back else X - 1 - i)
        for i in range(Z):
            wt[base + 8 + i] = decay(X * ((i - z - 1) if back else (z - 1 - i)))
        wt[base + 12] = decay((X - 1 - x) if back else x)
    once = jnp.exp(-r_rows)
    wt[26] = once
    wt[27] = coef_rows * once
    wt[28] = gain_rows

    def rows(b):
        return pl.ds(pl.multiple_of(b * L, L), L)

    def tile(b):
        return pl.ds(pl.multiple_of(b * C, C), C)

    def blocks(ch, body, batch=BATCH):
        def step(i, carry):
            stores = []
            for j in range(batch):
                stores += body(ch * per + i * batch + j)
            for ref, idx, value in stores:
                ref[idx] = value
            return carry

        lax.fori_loop(0, per // batch, step, 0)

    def row(ref, b):
        return ref[pl.ds(b, 1), :]

    def weight(i, b):
        return wt[i, pl.ds(b, 1), :]

    def big_rows(ch):
        return pl.ds(ch * per * L, per * L)

    def small_rows(ch):
        return pl.ds(ch * per * C, per * C)

    def f(ref, idx):
        return ref[idx, :].astype(F32)

    def squeeze_modes(full):
        return jnp.where(same, full, 0.0).reshape(G, C, L).sum(axis=0)

    def widen_modes(t):
        return jnp.where(same, jnp.concatenate([t] * G, axis=0), 0.0).astype(BF)

    def phase_a(ch):
        blocks(ch, lambda b: [
            (u1, rows(b), (f(q, rows(b)) * f(k, rows(b))).astype(BF))
        ])

    def halo(ch):
        part_rows = big_rows(ch)
        return remote(
            u1.at[part_rows], u1p.at[part_rows], halo_ss.at[ch], halo_rs.at[ch],
            seq=lax.rem(me + 1, nseq),
        )

    def halo_back(ch):
        part_rows = big_rows(ch)
        return remote(
            dz1.at[part_rows], dz1n.at[part_rows], halo2_ss.at[ch], halo2_rs.at[ch],
            seq=lax.rem(me + nseq - 1, nseq),
        )

    def row_copy(ref, ss, rsem, ch, d):
        return remote(
            ref.at[x, small_rows(ch)], ref.at[x, small_rows(ch)], ss.at[ch, d], rsem.at[ch, d],
            seq=z * X + lax.rem(x + d, X),
        )

    def z_copy(ref, ss, rsem, ch, d, sign):
        to = lax.rem(z + sign * d + Z, Z)
        return remote(
            ref.at[z, small_rows(ch)], ref.at[z, small_rows(ch)], ss.at[ch, d], rsem.at[ch, d],
            seq=to * X + x,
        )

    def phase_b(ch):
        def body(b):
            d2 = (f(go, rows(b)) * f(lv, rows(b))).astype(BF)
            r = row(r_s, b)
            powers = jnp.exp(-r * sub_f)
            high = powers.astype(BF)
            low = (powers - high.astype(F32)).astype(BF)
            amp = jnp.where(pick8, jnp.broadcast_to(row(coef_s, b), (G, L)), 0.0)
            amp_high = amp.astype(BF).astype(F32)
            amps = jnp.concatenate([amp_high, amp - amp_high], axis=0).astype(BF)
            h = dot(amps, high, NT) + dot(amps, low, NT)
            state = squeeze_modes(dot(d2, high, NN))
            return [
                (dz2, rows(b), d2),
                (tp, b, high),
                (tq, b, jnp.exp(-r * (L - 1.0 - sub_f)).astype(BF)),
                (h_s, octet(b), h[:G] + h[G:]),
                (row_b, (x, tile(b)), state.astype(BF)),
            ]

        blocks(ch, body)

    def octet(b):
        return pl.ds(pl.multiple_of(b * G, G), G)

    def circulant(line):
        return pltpu.roll(jnp.broadcast_to(line, (L, L)), 0, 1, stride=1, stride_axis=0)

    def phase_h(ch):
        def body(b):
            h = h_s[octet(b), :]
            d2 = dz2[rows(b), :]
            outs, stores = [], []
            for g in range(0, G, 2):
                mats = [
                    jnp.where(lower, circulant(h[g + i : g + i + 1]), 0.0).astype(BF)
                    for i in range(2)
                ]
                stores += [(hs, b * G + g + i, mats[i]) for i in range(2)]
                pair = dot(d2[g * C : (g + 2) * C], jnp.concatenate(mats, axis=0), NT)
                outs += [pair[:C, :L], pair[C:, L:]]
            return stores + [(du2, rows(b), jnp.concatenate(outs, axis=0))]

        blocks(ch, body, 2)

    def phase_t(ch):
        def body(b):
            lines = f_s[octet(b), :]
            stores = []
            for g in range(G):
                circ = circulant(lines[g : g + 1])
                mat = jnp.concatenate(
                    [jnp.where(lower, 0.0, circ), jnp.where(lower, circ, 0.0)], axis=0
                )
                stores.append((tw, b * G + g, mat.astype(BF)))
            return stores

        blocks(ch, body, 2)

    def mid(ch, rref, pref, zref, back):
        base = 13 * back

        def body(b):
            before = jnp.zeros((C, L), F32)
            whole = jnp.zeros((C, L), F32)
            for src in range(X):
                val = rref[src, tile(b), :].astype(F32)
                before = before + weight(base + src, b) * val
                whole = whole + weight(base + 4 + src, b) * val
            return [(pref, tile(b), before), (zref, (z, tile(b)), whole.astype(BF))]

        blocks(ch, body)

    def incoming(b, pref, zref, back):
        base = 13 * back
        acc = jnp.zeros((C, L), F32)
        for src in range(Z):
            gap = (src - z - 1) if back else (z - 1 - src)
            val = zref[src, tile(b), :].astype(F32)
            acc = acc + jnp.where(gap >= 0, weight(base + 8 + src, b) * val, 0.0)
        return pref[tile(b), :] + weight(base + 12, b) * acc

    def scaled(b, state):
        return widen_modes(weight(27, b) * state)

    def phase_bz(ch):
        def body(b):
            state = incoming(b, pref_b, z_b, 1)
            full = du2[rows(b), :] + dot(scaled(b, state), tq[b], NT)
            return [
                (b_in, tile(b), state),
                (du2, rows(b), full),
                (dz1, rows(b), (full * f(lk, rows(b)) * f(v, rows(b))).astype(BF)),
            ]

        blocks(ch, body)

    def phase_u(ch):
        def body(b):
            wide = jnp.concatenate([u1p[rows(b), :], u1[rows(b), :]], axis=1)
            outs = []
            for g in range(0, G, 2):
                mats = jnp.concatenate([tw[b * G + g], tw[b * G + g + 1]], axis=1)
                pair = dot(wide[g * C : (g + 2) * C], mats, NN)
                outs += [pair[:C, :L], pair[C:, L:]]
            z1 = jnp.concatenate(outs, axis=0)
            y1 = (f(v, rows(b)) * z1).astype(BF).astype(F32)
            full = du2[rows(b), :]
            key = f(lk, rows(b))
            second = (y1 * key).astype(BF)
            state = squeeze_modes(dot(second, tq[b], NN))
            return [
                (glk, rows(b), (full * y1).astype(BF)),
                (gv, rows(b), (full * key * z1).astype(BF)),
                (u2, rows(b), second),
                (s_loc, tile(b), state),
                (row_s, (x, tile(b)), state.astype(BF)),
            ]

        blocks(ch, body)

    def fold(mat):
        return pltpu.roll(mat, 1, 1, stride=1, stride_axis=0).sum(axis=0, keepdims=True)

    unfold = ((sub + lane) % L == 0).astype(F32)

    def masked(flip):
        return jnp.concatenate([flip * group_mask[g] for g in range(G)], axis=0)

    def phase_e(ch):
        def body(b):
            flip = dot(rev, dz1[rows(b), :], NT).astype(BF)
            wide = jnp.concatenate([u1p[rows(b), :], u1[rows(b), :]], axis=1)
            energy = dot(masked(flip), wide, NN)
            sums = [
                fold(jnp.where(keep, energy[g * L : (g + 1) * L, L:], energy[g * L : (g + 1) * L, :L]))
                for g in range(G)
            ]
            return [(lag1, octet(b), jnp.concatenate(sums, axis=0))]

        blocks(ch, body, 2)

    def phase_r(ch):
        def pair(i, carry):
            two = [ch * per + 2 * i, ch * per + 2 * i + 1]
            flips = [masked(dot(rev, dz2[rows(b), :], NT).astype(BF)) for b in two]
            zero = jnp.zeros((L, L), BF)
            seconds = [u2[rows(b), :] for b in two]
            diag = jnp.concatenate(
                [
                    jnp.concatenate([seconds[0], zero], axis=1),
                    jnp.concatenate([zero, seconds[1]], axis=1),
                ],
                axis=0,
            )
            energy = dot(jnp.concatenate(flips, axis=1), diag, NN)
            for j, b in enumerate(two):
                sums = [
                    fold(jnp.where(keep, energy[g * L : (g + 1) * L, j * L : (j + 1) * L], 0.0))
                    for g in range(G)
                ]
                lag2[octet(b), :] = jnp.concatenate(sums, axis=0)
            return carry

        lax.fori_loop(0, per // 2, pair, 0)

    def phase_z(ch):
        def body(b):
            second = u2[rows(b), :]
            outs = []
            for g in range(0, G, 2):
                mats = jnp.concatenate([hs[b * G + g], hs[b * G + g + 1]], axis=1)
                pair = dot(second[g * C : (g + 2) * C], mats, NN)
                outs += [pair[:C, :L], pair[C:, L:]]
            return [(z2i, rows(b), jnp.concatenate(outs, axis=0))]

        blocks(ch, body)

    def phase_g():
        filt_sum = dot_exact(lag1[...], unfold, NN)
        part[:, 0:G, :] = filt_sum.reshape(nb, G, L)
        first = lane[:G] == 0

        def step(i, carry):
            for j in range(BATCH):
                b = i * BATCH + j
                lags = lag2[octet(b), :]
                rest = jnp.where(first, 0.0, lags)
                high = rest.astype(BF).astype(F32)
                both = jnp.concatenate([high, rest - high], axis=0).astype(BF)
                inner = dot(both, tq[b], NN)
                inner = weight(26, b) * (inner[:G] + inner[G:]) + lags[:, 0:1]
                inner = jnp.where(pick8, inner, 0.0).sum(axis=0, keepdims=True)
                cross = (s_loc[tile(b), :] * b_in[tile(b), :]).sum(axis=0, keepdims=True)
                res = weight(28, b) * (inner + weight(26, b) * cross)
                part[b, G : 2 * G, :] = jnp.broadcast_to(res, (G, L))
            return carry

        lax.fori_loop(0, nb // BATCH, step, 0)

    def phase_sz(ch):
        def body(b):
            state = incoming(b, pref_s, z_s, 0)
            full = z2i[rows(b), :] + dot(scaled(b, state), tp[b], NT)
            return [(glv, rows(b), (f(go, rows(b)) * full).astype(BF))]

        blocks(ch, body)

    def phase_d(ch):
        def body(b):
            wide = jnp.concatenate([dz1n[rows(b), :], dz1[rows(b), :]], axis=1)
            outs = []
            for g in range(0, G, 2):
                mats = jnp.concatenate(
                    [
                        jnp.concatenate([tw[b * G + g + i, :L], tw[b * G + g + i, L:]], axis=1)
                        for i in range(2)
                    ],
                    axis=0,
                )
                pair = dot(wide[g * C : (g + 2) * C], mats, NT)
                outs += [pair[:C, :L], pair[C:, L:]]
            du1 = jnp.concatenate(outs, axis=0)
            return [
                (gq, rows(b), (du1 * f(k, rows(b))).astype(BF)),
                (gk, rows(b), (du1 * f(q, rows(b))).astype(BF)),
            ]

        blocks(ch, body)

    def start_row(ref, ss, rsem, ch):
        for d in range(1, X):
            row_copy(ref, ss, rsem, ch, d).start()

    def wait_row(ref, ss, rsem, ch):
        for d in range(1, X):
            row_copy(ref, ss, rsem, ch, d).wait_recv()

    def z_there(d, sign):
        return (z + d < Z) if sign > 0 else (z - d >= 0)

    def z_from(d, sign):
        return (z - d >= 0) if sign > 0 else (z + d < Z)

    def start_z(ref, ss, rsem, ch, sign):
        for d in range(1, Z):
            @pl.when(z_there(d, sign))
            def _():
                z_copy(ref, ss, rsem, ch, d, sign).start()

    def wait_z(ref, ss, rsem, ch, sign):
        for d in range(1, Z):
            @pl.when(z_from(d, sign))
            def _():
                z_copy(ref, ss, rsem, ch, d, sign).wait_recv()

    results = ((gq, gq_h), (gk, gk_h), (gv, gv_h), (glk, glk_h), (glv, glv_h))

    def save(i, ch):
        src, dst = results[i]
        part_rows = big_rows(ch)
        return pltpu.make_async_copy(src.at[part_rows], dst.at[part_rows], out_sem.at[i, ch])

    every = range(CHUNKS)

    @pl.when(me == 0)
    def _():
        u1p[...] = jnp.zeros_like(u1p)

    @pl.when(me == nseq - 1)
    def _():
        dz1n[...] = jnp.zeros_like(dz1n)

    loads[0].wait()
    loads[1].wait()
    for ch in every:
        phase_a(ch)
    pl.semaphore_wait(barrier, nseq)
    for ch in every:
        @pl.when(me < nseq - 1)
        def _():
            halo(ch).start()
    loads[2].wait()
    loads[3].wait()
    for ch in every:
        phase_b(ch)
        start_row(row_b, xb_ss, xb_rs, ch)
    for ch in every:
        phase_h(ch)
    for ch in every:
        wait_row(row_b, xb_ss, xb_rs, ch)
        mid(ch, row_b, pref_b, z_b, 1)
        start_z(z_b, zb_ss, zb_rs, ch, -1)
    for ch in every:
        phase_t(ch)
    loads[4].wait()
    loads[5].wait()
    for ch in every:
        wait_z(z_b, zb_ss, zb_rs, ch, -1)
        phase_bz(ch)
        @pl.when(me > 0)
        def _():
            halo_back(ch).start()
    for ch in every:
        @pl.when(me > 0)
        def _():
            halo(ch).wait_recv()
        phase_u(ch)
        start_row(row_s, xs_ss, xs_rs, ch)
        save(2, ch).start()
        save(3, ch).start()
    for ch in every:
        phase_e(ch)
        phase_r(ch)
    phase_g()
    for d in range(1, nseq):
        to = lax.rem(me + d, nseq)
        remote(part.at[to], rs.at[me], rs_ss.at[d], rs_rs.at[d], seq=to).start()
    for ch in every:
        wait_row(row_s, xs_ss, xs_rs, ch)
        mid(ch, row_s, pref_s, z_s, 0)
        start_z(z_s, zs_ss, zs_rs, ch, 1)
    for ch in every:
        phase_z(ch)
    rs[me] = part[me]
    for d in range(1, nseq):
        to = lax.rem(me + d, nseq)
        remote(part.at[to], rs.at[me], rs_ss.at[d], rs_rs.at[d], seq=to).wait_recv()
    own = rs[0]
    for i in range(1, nseq):
        own = own + rs[i]
    dpx[0] = own
    swap = remote(dpx.at[0], dpx.at[1], dp_ss, dp_rs, dp=1 - dp)
    swap.start()
    for ch in every:
        wait_z(z_s, zs_ss, zs_rs, ch, 1)
        phase_sz(ch)
        save(4, ch).start()
    swap.wait_recv()
    total[me] = dpx[0] + dpx[1]
    for d in range(1, nseq):
        to = lax.rem(me + d, nseq)
        remote(total.at[me], total.at[me], ag_ss.at[d], ag_rs.at[d], seq=to).start()
    for ch in every:
        @pl.when(me < nseq - 1)
        def _():
            halo_back(ch).wait_recv()
        phase_d(ch)
        save(0, ch).start()
        save(1, ch).start()
    for d in range(1, nseq):
        to = lax.rem(me + d, nseq)
        remote(total.at[me], total.at[me], ag_ss.at[d], ag_rs.at[d], seq=to).wait_recv()
    final = total[...]
    gf_o[...] = final[:, :G, :].reshape(nb * G, L)
    gr_o[...] = dot_exact(
        sel, jnp.where(spread, final[:, G:, :].reshape(nb * G, L), 0.0), NT
    )

    for ch in every:
        @pl.when(me < nseq - 1)
        def _():
            halo(ch).wait_send()

        @pl.when(me > 0)
        def _():
            halo_back(ch).wait_send()

        for d in range(1, X):
            row_copy(row_b, xb_ss, xb_rs, ch, d).wait_send()
            row_copy(row_s, xs_ss, xs_rs, ch, d).wait_send()
        for d in range(1, Z):
            @pl.when(z_there(d, -1))
            def _():
                z_copy(z_b, zb_ss, zb_rs, ch, d, -1).wait_send()

            @pl.when(z_there(d, 1))
            def _():
                z_copy(z_s, zs_ss, zs_rs, ch, d, 1).wait_send()

        for i in range(5):
            save(i, ch).wait()
    swap.wait_send()
    for d in range(1, nseq):
        to = lax.rem(me + d, nseq)
        remote(part.at[to], rs.at[me], rs_ss.at[d], rs_rs.at[d], seq=to).wait_send()
        remote(total.at[me], total.at[me], ag_ss.at[d], ag_rs.at[d], seq=to).wait_send()


def save_kernel(*refs):
    sems = refs[14]
    copies = [pltpu.make_async_copy(refs[i], refs[7 + i], sems.at[i]) for i in range(7)]
    for copy in copies:
        copy.start()
    for copy in copies:
        copy.wait()


def per_device(nseq, q, k, v, lk, lv, go, filt, resid, rate):
    channels = q.shape[1]
    groups = filt.shape[0]
    nb = channels // L
    Z = nseq // X
    big = jax.ShapeDtypeStruct((channels, L), BF)
    hbm = pl.BlockSpec(memory_space=pl.ANY)
    vmem = pl.BlockSpec(memory_space=pltpu.VMEM)
    dma = pltpu.SemaphoreType.DMA
    bigs = [pltpu.VMEM((channels, L), BF)]
    outs = pl.pallas_call(
        functools.partial(kernel, nseq),
        out_shape=[big] * 5
        + [jax.ShapeDtypeStruct((groups, L), F32), jax.ShapeDtypeStruct((C, groups), F32)],
        in_specs=[pl.BlockSpec(memory_space=pltpu.HBM)] * 6 + [vmem] * 3,
        out_specs=[hbm] * 5 + [vmem] * 2,
        scratch_shapes=bigs * 11
        + bigs * 6
        + [pltpu.VMEM((channels, L), F32)] * 2
        + [pltpu.VMEM((nb, L, L), BF)] * 2
        + [pltpu.VMEM((groups, L, L), BF), pltpu.VMEM((groups, 2 * L, L), BF)]
        + [pltpu.VMEM((groups, L), F32)] * 4
        + [pltpu.VMEM((nb, L), F32)] * 3
        + [pltpu.VMEM((WEIGHTS, nb, L), F32)]
        + [pltpu.VMEM((nb * C, L), F32)] * 4
        + [pltpu.VMEM((X, nb * C, L), BF)] * 2
        + [pltpu.VMEM((Z, nb * C, L), BF)] * 2
        + [pltpu.VMEM((nseq, 2 * G, L), F32)] * 2
        + [pltpu.VMEM((2, 2 * G, L), F32), pltpu.VMEM((nseq, 2 * G, L), F32)]
        + [dma((6,)), dma((5, CHUNKS))]
        + [dma((CHUNKS,))] * 4
        + [dma((CHUNKS, X))] * 2
        + [dma((CHUNKS, Z))] * 2
        + [dma((CHUNKS, X))] * 2
        + [dma((CHUNKS, Z))] * 2
        + [dma((nseq,))] * 2
        + [dma, dma]
        + [dma((nseq,))] * 2,
        compiler_params=pltpu.CompilerParams(
            collective_id=0, has_side_effects=True, vmem_limit_bytes=32 * 1024 * 1024
        ),
        name="hyena_bwd",
    )(
        *[pltpu.with_memory_space_constraint(a[0], pltpu.HBM) for a in (q, k, v, lk, lv, go)],
        filt, resid.T, rate.T,
    )
    outs = pl.pallas_call(
        save_kernel,
        out_shape=[jax.ShapeDtypeStruct(o.shape, o.dtype) for o in outs],
        in_specs=[vmem] * 7,
        out_specs=[hbm] * 7,
        scratch_shapes=[dma((7,))],
        compiler_params=pltpu.CompilerParams(vmem_limit_bytes=16 * 1024 * 1024),
        name="hyena_save",
    )(*outs)
    return tuple(o[None] for o in outs[:5]) + (outs[5], outs[6].T)


def solution(mesh):
    wide = P("dp", "chan", "seq")
    small = P("chan", None)
    return jax.shard_map(
        functools.partial(per_device, mesh.shape["seq"]),
        mesh=mesh,
        in_specs=(wide,) * 6 + (small,) * 3,
        out_specs=(wide,) * 5 + (small,) * 2,
        check_vma=False,
    )
```

```python
import functools

import jax
import jax.numpy as jnp
from jax import lax
from jax.experimental import pallas as pl
from jax.experimental.pallas import tpu as pltpu
from jax.sharding import PartitionSpec as P

MESH = pl.DeviceIdType.MESH
NN = (((1,), (0,)), ((), ()))
NT = (((1,), (1,)), ((), ()))
TN = (((0,), (0,)), ((), ()))
EXACT = lax.Precision.HIGHEST
BF = jnp.bfloat16
F32 = jnp.float32

L = 128
C = 16
G = 8
X = 4
CHUNKS = 2
BATCH = 8
PIECES = 2
WEIGHTS = 20


def dot(a, b, dims):
    return lax.dot_general(a, b, dims, preferred_element_type=F32)


def dot_exact(a, b, dims):
    return lax.dot_general(a, b, dims, precision=EXACT, preferred_element_type=F32)


def one_minus_exp_neg(x):
    acc = jnp.full_like(x, 1.0 / 40320.0)
    for divisor in (5040.0, 720.0, 120.0, 24.0, 6.0, 2.0, 1.0):
        acc = 1.0 / divisor - x * acc
    return x * acc


def kernel(
    nseq, q_h, k_h, v_h, lk_h, lv_h, go_h, filt_h, resid_h, rate_h,
    gq_h, gk_h, gv_h, glk_h, glv_h, gf_o, gr_o,
    filt, resid, rate, q, k, v, lk, lv, go, gq, gk, gv, glk, glv,
    u1, u1p, dz2, dz1, dz1n, u2, du2, z2i,
    tp, tq, hs, tw, h_s, f_s, lag1, lag2,
    r_s, coef_s, gain_s, wt, s_loc, b_in, tc_b, tc_s,
    row_b, row_s, z_b, z_s, part, rs, dpx, total, y1_s, z1_s, res, res_dp, res_all,
    in_sem, out_sem, halo_ss, halo_rs, halo2_ss, halo2_rs,
    xb_ss, xb_rs, zb_ss, zb_rs, xs_ss, xs_rs, zs_ss, zs_rs,
    rs_ss, rs_rs, dp_ss, dp_rs, ag_ss, ag_rs, rd_ss, rd_rs, ra_ss, ra_rs,
):
    channels = q.shape[0]
    nb = channels // L
    per = nb // CHUNKS
    Z = nseq // X
    me = lax.axis_index("seq")
    dp = lax.axis_index("dp")
    z = me // X
    x = me - z * X

    ins = (
        (rate_h, rate), (resid_h, resid), (go_h, go), (lv_h, lv),
        (q_h, q), (k_h, k), (filt_h, filt), (lk_h, lk), (v_h, v),
    )
    loads = [pltpu.make_async_copy(s, d, in_sem.at[i]) for i, (s, d) in enumerate(ins)]
    for load in loads:
        load.start()

    barrier = pltpu.get_barrier_semaphore()
    for d in range(1, nseq):
        pl.semaphore_signal(
            barrier, inc=1, device_id={"seq": lax.rem(me + d, nseq)}, device_id_type=MESH
        )
    pl.semaphore_signal(barrier, inc=1, device_id={"dp": 1 - dp}, device_id_type=MESH)

    def remote(src, dst, ss, rsem, **where):
        return pltpu.make_async_remote_copy(
            src_ref=src, dst_ref=dst, send_sem=ss, recv_sem=rsem,
            device_id=where, device_id_type=MESH,
        )

    sub = lax.broadcasted_iota(jnp.int32, (L, L), 0)
    lane = lax.broadcasted_iota(jnp.int32, (L, L), 1)
    sub_f = sub.astype(F32)
    same = (sub // C) == (lane // C)
    lower = lane >= sub
    rev = (sub + lane == L - 1).astype(F32).astype(BF)
    keep = sub + lane <= L - 1
    pick8 = lax.broadcasted_iota(jnp.int32, (G, L), 1) // C == lax.broadcasted_iota(
        jnp.int32, (G, L), 0
    )
    lane_group = lax.broadcasted_iota(jnp.int32, (1, L), 1) // C
    group_mask = [(lane_group == g).astype(F32).astype(BF) for g in range(G)]

    loads[0].wait()
    loads[1].wait()
    sel = (
        lax.broadcasted_iota(jnp.int32, (C, L), 1) % C
        == lax.broadcasted_iota(jnp.int32, (C, L), 0)
    ).astype(F32)
    spread = ((sub % G) == (lane // C))

    def to_rows(mat):
        wide = dot_exact(mat, sel, TN)
        return jnp.where(spread, wide, 0.0).reshape(nb, G, L).sum(axis=1)

    r_rows = to_rows(rate[...])
    gain_rows = jnp.sqrt(one_minus_exp_neg(2.0 * r_rows))
    r_s[...] = r_rows
    gain_s[...] = gain_rows
    coef_rows = to_rows(resid[...]) * gain_rows
    coef_s[...] = coef_rows

    def decay(steps):
        if isinstance(steps, int):
            return jnp.exp(-r_rows * float(L * steps))
        ok = steps >= 0
        return jnp.where(ok, jnp.exp(-r_rows * (L * jnp.maximum(steps, 0)).astype(F32)), 0.0)

    for back in (0, 1):
        for i in range(X):
            ahead = (i > x) if back else (i < x)
            near = (i - x - 1) if back else (x - 1 - i)
            wt[8 * back + i] = decay(jnp.where(ahead, near, near + X))
        for i in range(Z):
            wt[8 * back + X + i] = decay(X * ((i - z - 1) if back else (z - 1 - i)))
    once = jnp.exp(-r_rows)
    wt[16] = decay(X)
    wt[17] = once
    wt[18] = coef_rows * once
    wt[19] = gain_rows

    def rows(b):
        return pl.ds(pl.multiple_of(b * L, L), L)

    def tile(b):
        return pl.ds(pl.multiple_of(b * C, C), C)

    def blocks(ch, body, batch=BATCH):
        def step(i, carry):
            stores = []
            for j in range(batch):
                stores += body(ch * per + i * batch + j)
            for ref, idx, value in stores:
                ref[idx] = value
            return carry

        lax.fori_loop(0, per // batch, step, 0)

    def row(ref, b):
        return ref[pl.ds(b, 1), :]

    def weight(i, b):
        return wt[i, pl.ds(b, 1), :]

    def big_rows(ch):
        return pl.ds(ch * per * L, per * L)

    def small_rows(ch):
        return pl.ds(ch * per * C, per * C)

    def f(ref, idx):
        return ref[idx, :].astype(F32)

    def squeeze_modes(full):
        return jnp.where(same, full, 0.0).reshape(G, C, L).sum(axis=0)

    def widen_modes(t):
        return jnp.where(same, jnp.concatenate([t] * G, axis=0), 0.0).astype(BF)

    def phase_a(ch):
        blocks(ch, lambda b: [
            (u1, rows(b), (f(q, rows(b)) * f(k, rows(b))).astype(BF))
        ])

    def piece_rows(i):
        return pl.ds(i * (per // PIECES) * L, (per // PIECES) * L)

    def halo(i):
        part_rows = piece_rows(i)
        return remote(
            u1.at[part_rows], u1p.at[part_rows], halo_ss.at[i], halo_rs.at[i],
            seq=lax.rem(me + 1, nseq),
        )

    def halo_back(i):
        part_rows = piece_rows(i)
        return remote(
            dz1.at[part_rows], dz1n.at[part_rows], halo2_ss.at[i], halo2_rs.at[i],
            seq=lax.rem(me + nseq - 1, nseq),
        )

    def x_copy(both, ref, ss, rsem, ch, d, sign):
        to = lax.rem(x + d, X)
        inclusive = jnp.where((to > x) if sign > 0 else (to < x), 1, 0)
        return remote(
            both.at[inclusive, small_rows(ch)], ref.at[x, small_rows(ch)],
            ss.at[ch, d], rsem.at[ch, d], seq=z * X + to,
        )

    def z_copy(ref, ss, rsem, ch, d, sign):
        to = lax.rem(z + sign * d + Z, Z)
        return remote(
            ref.at[z, small_rows(ch)], ref.at[z, small_rows(ch)], ss.at[ch, d], rsem.at[ch, d],
            seq=to * X + x,
        )

    def phase_b(ch):
        def body(b):
            d2 = (f(go, rows(b)) * f(lv, rows(b))).astype(BF)
            r = row(r_s, b)
            powers = jnp.exp(-r * sub_f)
            high = powers.astype(BF)
            low = (powers - high.astype(F32)).astype(BF)
            amp = jnp.where(pick8, jnp.broadcast_to(row(coef_s, b), (G, L)), 0.0)
            amp_high = amp.astype(BF).astype(F32)
            amps = jnp.concatenate([amp_high, amp - amp_high], axis=0).astype(BF)
            h = dot(amps, high, NT) + dot(amps, low, NT)
            state = squeeze_modes(dot(d2, high, NN))
            return [
                (dz2, rows(b), d2),
                (tp, b, high),
                (tq, b, jnp.exp(-r * (L - 1.0 - sub_f)).astype(BF)),
                (h_s, octet(b), h[:G] + h[G:]),
                (z_b, (z, tile(b)), state.astype(BF)),
            ]

        blocks(ch, body)

    def octet(b):
        return pl.ds(pl.multiple_of(b * G, G), G)

    def circulant(line):
        return pltpu.roll(jnp.broadcast_to(line, (L, L)), 0, 1, stride=1, stride_axis=0)

    def phase_h(ch):
        def body(b):
            h = h_s[octet(b), :]
            d2 = dz2[rows(b), :]
            outs, stores = [], []
            for g in range(0, G, 2):
                mats = [
                    jnp.where(lower, circulant(h[g + i : g + i + 1]), 0.0).astype(BF)
                    for i in range(2)
                ]
                stores += [(hs, b * G + g + i, mats[i]) for i in range(2)]
                pair = dot(d2[g * C : (g + 2) * C], jnp.concatenate(mats, axis=0), NT)
                outs += [pair[:C, :L], pair[C:, L:]]
            return stores + [(du2, rows(b), jnp.concatenate(outs, axis=0))]

        blocks(ch, body, 4)

    def phase_t(ch):
        def body(b):
            lines = f_s[octet(b), :]
            stores = []
            for g in range(G):
                circ = circulant(lines[g : g + 1])
                mat = jnp.concatenate(
                    [jnp.where(lower, 0.0, circ), jnp.where(lower, circ, 0.0)], axis=0
                )
                stores.append((tw, b * G + g, mat.astype(BF)))
            return stores

        blocks(ch, body, 4)

    def mid(ch, zref, both, rref, back):
        def body(b):
            acc = jnp.zeros((C, L), F32)
            for src in range(Z):
                gap = (src - z - 1) if back else (z - 1 - src)
                val = zref[src, tile(b), :].astype(F32)
                acc = acc + jnp.where(gap >= 0, weight(8 * back + X + src, b) * val, 0.0)
            whole = zref[z, tile(b), :].astype(F32) + weight(16, b) * acc
            acc = acc.astype(BF)
            return [
                (both, (0, tile(b)), acc),
                (both, (1, tile(b)), whole.astype(BF)),
                (rref, (x, tile(b)), acc),
            ]

        blocks(ch, body)

    def incoming(b, rref, back):
        acc = jnp.zeros((C, L), F32)
        for src in range(X):
            acc = acc + weight(8 * back + src, b) * rref[src, tile(b), :].astype(F32)
        return acc

    def scaled(b, state):
        return widen_modes(weight(18, b) * state)

    def phase_bz(ch):
        def body(b):
            state = incoming(b, row_b, 1)
            full = du2[rows(b), :] + dot(scaled(b, state), tq[b], NT)
            return [
                (b_in, tile(b), state),
                (du2, rows(b), full),
                (dz1, rows(b), (full * f(lk, rows(b)) * f(v, rows(b))).astype(BF)),
            ]

        blocks(ch, body)

    def phase_k(ch):
        def body(b):
            full = du2[rows(b), :]
            return [
                (glk, rows(b), (full * f(y1_s, rows(b))).astype(BF)),
                (gv, rows(b), (full * f(lk, rows(b)) * z1_s[rows(b), :]).astype(BF)),
            ]

        blocks(ch, body)

    def phase_u(ch):
        def body(b):
            wide = jnp.concatenate([u1p[rows(b), :], u1[rows(b), :]], axis=1)
            outs = []
            for g in range(0, G, 2):
                mats = jnp.concatenate([tw[b * G + g], tw[b * G + g + 1]], axis=1)
                pair = dot(wide[g * C : (g + 2) * C], mats, NN)
                outs += [pair[:C, :L], pair[C:, L:]]
            z1 = jnp.concatenate(outs, axis=0)
            y1 = (f(v, rows(b)) * z1).astype(BF)
            second = (y1.astype(F32) * f(lk, rows(b))).astype(BF)
            state = squeeze_modes(dot(second, tq[b], NN))
            return [
                (y1_s, rows(b), y1),
                (z1_s, rows(b), z1),
                (u2, rows(b), second),
                (s_loc, tile(b), state),
                (z_s, (z, tile(b)), state.astype(BF)),
            ]

        blocks(ch, body)

    def fold(mat):
        return pltpu.roll(mat, 1, 1, stride=1, stride_axis=0).sum(axis=0, keepdims=True)

    unfold = ((sub + lane) % L == 0).astype(F32)

    def masked(flip):
        return jnp.concatenate([flip * group_mask[g] for g in range(G)], axis=0)

    def phase_e(ch):
        def body(b):
            flip = dot(rev, dz1[rows(b), :], NT).astype(BF)
            wide = jnp.concatenate([u1p[rows(b), :], u1[rows(b), :]], axis=1)
            energy = dot(masked(flip), wide, NN)
            sums = [
                fold(jnp.where(keep, energy[g * L : (g + 1) * L, L:], energy[g * L : (g + 1) * L, :L]))
                for g in range(G)
            ]
            return [(lag1, octet(b), jnp.concatenate(sums, axis=0))]

        blocks(ch, body, 4)

    def phase_r(ch):
        def pair(i, carry):
            two = [ch * per + 2 * i, ch * per + 2 * i + 1]
            flips = [masked(dot(rev, dz2[rows(b), :], NT).astype(BF)) for b in two]
            zero = jnp.zeros((L, L), BF)
            seconds = [u2[rows(b), :] for b in two]
            diag = jnp.concatenate(
                [
                    jnp.concatenate([seconds[0], zero], axis=1),
                    jnp.concatenate([zero, seconds[1]], axis=1),
                ],
                axis=0,
            )
            energy = dot(jnp.concatenate(flips, axis=1), diag, NN)
            for j, b in enumerate(two):
                sums = [
                    fold(jnp.where(keep, energy[g * L : (g + 1) * L, j * L : (j + 1) * L], 0.0))
                    for g in range(G)
                ]
                lag2[octet(b), :] = jnp.concatenate(sums, axis=0)
            return carry

        lax.fori_loop(0, per // 2, pair, 0, unroll=2)

    def phase_z(ch):
        def body(b):
            second = u2[rows(b), :]
            outs = []
            for g in range(0, G, 2):
                mats = jnp.concatenate([hs[b * G + g], hs[b * G + g + 1]], axis=1)
                pair = dot(second[g * C : (g + 2) * C], mats, NN)
                outs += [pair[:C, :L], pair[C:, L:]]
            return [(z2i, rows(b), jnp.concatenate(outs, axis=0))]

        blocks(ch, body)

    def phase_gf():
        part[...] = dot_exact(lag1[...], unfold, NN).reshape(nb, G, L)

    def phase_gr():
        first = lane[:G] == 0

        def step(i, carry):
            values = []
            for j in range(BATCH):
                b = i * BATCH + j
                lags = lag2[octet(b), :]
                rest = jnp.where(first, 0.0, lags)
                high = rest.astype(BF).astype(F32)
                both = jnp.concatenate([high, rest - high], axis=0).astype(BF)
                inner = dot(both, tq[b], NN)
                inner = weight(17, b) * (inner[:G] + inner[G:]) + lags[:, 0:1]
                inner = jnp.where(pick8, inner, 0.0).sum(axis=0, keepdims=True)
                cross = (s_loc[tile(b), :] * b_in[tile(b), :]).sum(axis=0, keepdims=True)
                values.append(weight(19, b) * (inner + weight(17, b) * cross))
            for j in range(BATCH):
                res[pl.ds(i * BATCH + j, 1), :] = values[j]
            return carry

        lax.fori_loop(0, nb // BATCH, step, 0)

    def phase_sz(ch):
        def body(b):
            state = incoming(b, row_s, 0)
            full = z2i[rows(b), :] + dot(scaled(b, state), tp[b], NT)
            return [(glv, rows(b), (f(go, rows(b)) * full).astype(BF))]

        blocks(ch, body)

    def phase_d(ch):
        def body(b):
            wide = jnp.concatenate([dz1n[rows(b), :], dz1[rows(b), :]], axis=1)
            outs = []
            for g in range(0, G, 2):
                mats = jnp.concatenate(
                    [
                        jnp.concatenate([tw[b * G + g + i, :L], tw[b * G + g + i, L:]], axis=1)
                        for i in range(2)
                    ],
                    axis=0,
                )
                pair = dot(wide[g * C : (g + 2) * C], mats, NT)
                outs += [pair[:C, :L], pair[C:, L:]]
            du1 = jnp.concatenate(outs, axis=0)
            return [
                (gq, rows(b), (du1 * f(k, rows(b))).astype(BF)),
                (gk, rows(b), (du1 * f(q, rows(b))).astype(BF)),
            ]

        blocks(ch, body)

    def start_x(both, ref, ss, rsem, ch, sign):
        for d in range(1, X):
            x_copy(both, ref, ss, rsem, ch, d, sign).start()

    def wait_x(both, ref, ss, rsem, ch, sign):
        for d in range(1, X):
            x_copy(both, ref, ss, rsem, ch, d, sign).wait_recv()

    def z_there(d, sign):
        return (z + d < Z) if sign > 0 else (z - d >= 0)

    def z_from(d, sign):
        return (z - d >= 0) if sign > 0 else (z + d < Z)

    def start_z(ref, ss, rsem, ch, sign):
        for d in range(1, Z):
            @pl.when(z_there(d, sign))
            def _():
                z_copy(ref, ss, rsem, ch, d, sign).start()

    def wait_z(ref, ss, rsem, ch, sign):
        for d in range(1, Z):
            @pl.when(z_from(d, sign))
            def _():
                z_copy(ref, ss, rsem, ch, d, sign).wait_recv()

    results = ((gq, gq_h), (gk, gk_h), (gv, gv_h), (glk, glk_h), (glv, glv_h))

    def save(i, ch):
        src, dst = results[i]
        part_rows = big_rows(ch)
        return pltpu.make_async_copy(src.at[part_rows], dst.at[part_rows], out_sem.at[i, ch])

    every = range(CHUNKS)

    @pl.when(me == 0)
    def _():
        u1p[...] = jnp.zeros_like(u1p)

    @pl.when(me == nseq - 1)
    def _():
        dz1n[...] = jnp.zeros_like(dz1n)

    def peer(d):
        return lax.rem(me + d, nseq)

    def scatter(d):
        return remote(part.at[peer(d)], rs.at[me], rs_ss.at[d], rs_rs.at[d], seq=peer(d))

    def gather(d):
        return remote(total.at[me], total.at[me], ag_ss.at[d], ag_rs.at[d], seq=peer(d))

    def gather_res(d):
        return remote(res_all.at[me], res_all.at[me], ra_ss.at[d], ra_rs.at[d], seq=peer(d))

    swap = remote(dpx.at[0], dpx.at[1], dp_ss, dp_rs, dp=1 - dp)
    swap_res = remote(res, res_dp, rd_ss, rd_rs, dp=1 - dp)
    peers = range(1, nseq)

    def send_halo(ch):
        for i in range(ch * PIECES, (ch + 1) * PIECES):
            @pl.when(me < nseq - 1)
            def _():
                halo(i).start()

    def send_back(ch):
        for i in range(ch * PIECES, (ch + 1) * PIECES):
            @pl.when(me > 0)
            def _():
                halo_back(i).start()

    def run_u(ch):
        for i in range(ch * PIECES, (ch + 1) * PIECES):
            @pl.when(me > 0)
            def _():
                halo(i).wait_recv()
        phase_u(ch)
        start_z(z_s, zs_ss, zs_rs, ch, 1)

    def run_bz(ch):
        wait_x(tc_b, row_b, xb_ss, xb_rs, ch, -1)
        phase_bz(ch)
        send_back(ch)

    def run_mid_b(ch):
        wait_z(z_b, zb_ss, zb_rs, ch, -1)
        mid(ch, z_b, tc_b, row_b, 1)
        start_x(tc_b, row_b, xb_ss, xb_rs, ch, -1)

    def run_mid_s(ch):
        wait_z(z_s, zs_ss, zs_rs, ch, 1)
        mid(ch, z_s, tc_s, row_s, 0)
        start_x(tc_s, row_s, xs_ss, xs_rs, ch, 1)

    def run_d(ch):
        for i in range(ch * PIECES, (ch + 1) * PIECES):
            @pl.when(me < nseq - 1)
            def _():
                halo_back(i).wait_recv()
        phase_d(ch)
        save(0, ch).start()
        save(1, ch).start()

    def run_sz(ch):
        wait_x(tc_s, row_s, xs_ss, xs_rs, ch, 1)
        phase_sz(ch)
        save(4, ch).start()

    def run_k(ch):
        phase_k(ch)
        save(2, ch).start()
        save(3, ch).start()

    loads[2].wait()
    loads[3].wait()
    for ch in every:
        phase_b(ch)
    loads[4].wait()
    loads[5].wait()
    for ch in every:
        phase_a(ch)
    pl.semaphore_wait(barrier, nseq)
    for ch in every:
        start_z(z_b, zb_ss, zb_rs, ch, -1)
    send_halo(0)
    loads[6].wait()
    f_s[...] = filt[...].astype(F32)
    for ch in every:
        phase_h(ch)
    phase_t(0)
    for ch in every:
        run_mid_b(ch)
    for ch in range(1, CHUNKS):
        send_halo(ch)
    for ch in range(1, CHUNKS):
        phase_t(ch)
    loads[7].wait()
    loads[8].wait()
    run_u(0)
    for ch in every:
        run_bz(ch)
    phase_e(0)
    run_mid_s(0)
    phase_r(0)
    for ch in range(1, CHUNKS):
        run_u(ch)
        phase_e(ch)
    phase_gf()
    for d in peers:
        scatter(d).start()
    for ch in range(1, CHUNKS):
        run_mid_s(ch)
        phase_r(ch)
    phase_gr()
    swap_res.start()
    rs[me] = part[me]
    for d in peers:
        scatter(d).wait_recv()
    own = rs[0]
    for i in range(1, nseq):
        own = own + rs[i]
    dpx[0] = own
    swap.start()
    for ch in every:
        run_k(ch)
    swap_res.wait_recv()
    res_all[me] = res[...] + res_dp[...]
    for d in peers:
        gather_res(d).start()
    swap.wait_recv()
    total[me] = dpx[0] + dpx[1]
    for d in peers:
        gather(d).start()
    for ch in every:
        phase_z(ch)
    for ch in every:
        run_d(ch)
    for ch in every:
        run_sz(ch)
    for d in peers:
        gather(d).wait_recv()
    gf_o[...] = total[...].reshape(nb * G, L)
    for d in peers:
        gather_res(d).wait_recv()
    res_sum = res_all[0]
    for i in range(1, nseq):
        res_sum = res_sum + res_all[i]
    wide = jnp.broadcast_to(res_sum[:, None, :], (nb, G, L)).reshape(nb * G, L)
    gr_o[...] = dot_exact(sel, jnp.where(spread, wide, 0.0), NT)

    for i in range(CHUNKS * PIECES):
        @pl.when(me < nseq - 1)
        def _():
            halo(i).wait_send()

        @pl.when(me > 0)
        def _():
            halo_back(i).wait_send()

    for ch in every:
        for d in range(1, X):
            x_copy(tc_b, row_b, xb_ss, xb_rs, ch, d, -1).wait_send()
            x_copy(tc_s, row_s, xs_ss, xs_rs, ch, d, 1).wait_send()
        for d in range(1, Z):
            @pl.when(z_there(d, -1))
            def _():
                z_copy(z_b, zb_ss, zb_rs, ch, d, -1).wait_send()

            @pl.when(z_there(d, 1))
            def _():
                z_copy(z_s, zs_ss, zs_rs, ch, d, 1).wait_send()

        for i in range(5):
            save(i, ch).wait()
    swap.wait_send()
    swap_res.wait_send()
    for d in peers:
        scatter(d).wait_send()
        gather(d).wait_send()
        gather_res(d).wait_send()


def save_kernel(*refs):
    sems = refs[14]
    copies = [pltpu.make_async_copy(refs[i], refs[7 + i], sems.at[i]) for i in range(7)]
    for copy in copies:
        copy.start()
    for copy in copies:
        copy.wait()


def per_device(nseq, q, k, v, lk, lv, go, filt, resid, rate):
    channels = q.shape[1]
    groups = filt.shape[0]
    nb = channels // L
    Z = nseq // X
    big = jax.ShapeDtypeStruct((channels, L), BF)
    hbm = pl.BlockSpec(memory_space=pl.ANY)
    vmem = pl.BlockSpec(memory_space=pltpu.VMEM)
    dma = pltpu.SemaphoreType.DMA
    bigs = [pltpu.VMEM((channels, L), BF)]
    outs = pl.pallas_call(
        functools.partial(kernel, nseq),
        out_shape=[big] * 5
        + [jax.ShapeDtypeStruct((groups, L), F32), jax.ShapeDtypeStruct((C, groups), F32)],
        in_specs=[pl.BlockSpec(memory_space=pltpu.HBM)] * 9,
        out_specs=[hbm] * 5 + [vmem] * 2,
        scratch_shapes=[
            pltpu.VMEM((groups, L), BF),
            pltpu.VMEM((C, groups), F32),
            pltpu.VMEM((C, groups), F32),
        ]
        + bigs * 11
        + bigs * 6
        + [pltpu.VMEM((channels, L), F32)] * 2
        + [pltpu.VMEM((nb, L, L), BF)] * 2
        + [pltpu.VMEM((groups, L, L), BF), pltpu.VMEM((groups, 2 * L, L), BF)]
        + [pltpu.VMEM((groups, L), F32)] * 4
        + [pltpu.VMEM((nb, L), F32)] * 3
        + [pltpu.VMEM((WEIGHTS, nb, L), F32)]
        + [pltpu.VMEM((nb * C, L), F32)] * 2
        + [pltpu.VMEM((2, nb * C, L), BF)] * 2
        + [pltpu.VMEM((X, nb * C, L), BF)] * 2
        + [pltpu.VMEM((Z, nb * C, L), BF)] * 2
        + [pltpu.VMEM((nseq, G, L), F32)] * 2
        + [pltpu.VMEM((2, G, L), F32), pltpu.VMEM((nseq, G, L), F32)]
        + [pltpu.VMEM((channels, L), BF), pltpu.VMEM((channels, L), F32)]
        + [pltpu.VMEM((nb, L), F32)] * 2
        + [pltpu.VMEM((nseq, nb, L), F32)]
        + [dma((9,)), dma((5, CHUNKS))]
        + [dma((CHUNKS * PIECES,))] * 4
        + [dma((CHUNKS, X))] * 2
        + [dma((CHUNKS, Z))] * 2
        + [dma((CHUNKS, X))] * 2
        + [dma((CHUNKS, Z))] * 2
        + [dma((nseq,))] * 2
        + [dma, dma]
        + [dma((nseq,))] * 2
        + [dma, dma]
        + [dma((nseq,))] * 2,
        compiler_params=pltpu.CompilerParams(
            collective_id=0, has_side_effects=True, vmem_limit_bytes=32 * 1024 * 1024
        ),
        name="hyena_bwd",
    )(
        *[
            pltpu.with_memory_space_constraint(a, pltpu.HBM)
            for a in (q[0], k[0], v[0], lk[0], lv[0], go[0], filt, resid.T, rate.T)
        ]
    )
    outs = pl.pallas_call(
        save_kernel,
        out_shape=[jax.ShapeDtypeStruct(o.shape, o.dtype) for o in outs],
        in_specs=[vmem] * 7,
        out_specs=[hbm] * 7,
        scratch_shapes=[dma((7,))],
        compiler_params=pltpu.CompilerParams(vmem_limit_bytes=16 * 1024 * 1024),
        name="hyena_save",
    )(*outs)
    return tuple(o[None] for o in outs[:5]) + (outs[5], outs[6].T)


def solution(mesh):
    wide = P("dp", "chan", "seq")
    small = P("chan", None)
    return jax.shard_map(
        functools.partial(per_device, mesh.shape["seq"]),
        mesh=mesh,
        in_specs=(wide,) * 6 + (small,) * 3,
        out_specs=(wide,) * 5 + (small,) * 2,
        check_vma=False,
    )
```

```python
import functools

import jax
import jax.numpy as jnp
from jax import lax
from jax.experimental import pallas as pl
from jax.experimental.pallas import tpu as pltpu
from jax.sharding import PartitionSpec as P

MESH = pl.DeviceIdType.MESH
NN = (((1,), (0,)), ((), ()))
NT = (((1,), (1,)), ((), ()))
TN = (((0,), (0,)), ((), ()))
EXACT = lax.Precision.HIGHEST
BF = jnp.bfloat16
F32 = jnp.float32

L = 128
C = 16
G = 8
X = 4
CHUNKS = 2
BATCH = 8
PIECES = 2
WEIGHTS = 20


def dot(a, b, dims):
    return lax.dot_general(a, b, dims, preferred_element_type=F32)


def dot_exact(a, b, dims):
    return lax.dot_general(a, b, dims, precision=EXACT, preferred_element_type=F32)


def one_minus_exp_neg(x):
    acc = jnp.full_like(x, 1.0 / 40320.0)
    for divisor in (5040.0, 720.0, 120.0, 24.0, 6.0, 2.0, 1.0):
        acc = 1.0 / divisor - x * acc
    return x * acc


def kernel(
    nseq, q_h, k_h, v_h, lk_h, lv_h, go_h, filt_h, resid_h, rate_h,
    gq_h, gk_h, gv_h, glk_h, glv_h, gf_o, gr_o,
    filt, resid, rate, q, k, v, lk, lv, go, gq, gk, gv, glk, glv,
    u1, u1p, dz2, dz1, dz1n, u2, du2, z2i,
    tp, tq, hs, tw, h_s, f_s, lag1, lag2,
    r_s, coef_s, gain_s, wt, s_loc, b_in, tc_b, tc_s,
    row_b, row_s, z_b, z_s, part, rs, dpx, total, y1_s, z1_s, res, res_dp, res_all,
    in_sem, out_sem, halo_ss, halo_rs, halo2_ss, halo2_rs,
    xb_ss, xb_rs, zb_ss, zb_rs, xs_ss, xs_rs, zs_ss, zs_rs,
    rs_ss, rs_rs, dp_ss, dp_rs, ag_ss, ag_rs, rd_ss, rd_rs, ra_ss, ra_rs,
):
    channels = q.shape[0]
    nb = channels // L
    per = nb // CHUNKS
    Z = nseq // X
    me = lax.axis_index("seq")
    dp = lax.axis_index("dp")
    z = me // X
    x = me - z * X

    ins = (
        (q_h, q), (k_h, k), (rate_h, rate), (resid_h, resid), (go_h, go),
        (lv_h, lv), (filt_h, filt), (lk_h, lk), (v_h, v),
    )
    loads = [pltpu.make_async_copy(s, d, in_sem.at[i]) for i, (s, d) in enumerate(ins)]
    for load in loads:
        load.start()

    barrier = pltpu.get_barrier_semaphore()
    for d in range(1, nseq):
        pl.semaphore_signal(
            barrier, inc=1, device_id={"seq": lax.rem(me + d, nseq)}, device_id_type=MESH
        )
    pl.semaphore_signal(barrier, inc=1, device_id={"dp": 1 - dp}, device_id_type=MESH)

    def remote(src, dst, ss, rsem, **where):
        return pltpu.make_async_remote_copy(
            src_ref=src, dst_ref=dst, send_sem=ss, recv_sem=rsem,
            device_id=where, device_id_type=MESH,
        )

    sub = lax.broadcasted_iota(jnp.int32, (L, L), 0)
    lane = lax.broadcasted_iota(jnp.int32, (L, L), 1)
    sub_f = sub.astype(F32)
    same = (sub // C) == (lane // C)
    lower = lane >= sub
    rev = (sub + lane == L - 1).astype(F32).astype(BF)
    keep = sub + lane <= L - 1
    pick8 = lax.broadcasted_iota(jnp.int32, (G, L), 1) // C == lax.broadcasted_iota(
        jnp.int32, (G, L), 0
    )
    lane_group = lax.broadcasted_iota(jnp.int32, (1, L), 1) // C
    group_mask = [(lane_group == g).astype(F32).astype(BF) for g in range(G)]

    def rows(b):
        return pl.ds(pl.multiple_of(b * L, L), L)

    def tile(b):
        return pl.ds(pl.multiple_of(b * C, C), C)

    def blocks(ch, body, batch=BATCH):
        def step(i, carry):
            stores = []
            for j in range(batch):
                stores += body(ch * per + i * batch + j)
            for ref, idx, value in stores:
                ref[idx] = value
            return carry

        lax.fori_loop(0, per // batch, step, 0)

    def row(ref, b):
        return ref[pl.ds(b, 1), :]

    def weight(i, b):
        return wt[i, pl.ds(b, 1), :]

    def big_rows(ch):
        return pl.ds(ch * per * L, per * L)

    def small_rows(ch):
        return pl.ds(ch * per * C, per * C)

    def f(ref, idx):
        return ref[idx, :].astype(F32)

    def squeeze_modes(full):
        return jnp.where(same, full, 0.0).reshape(G, C, L).sum(axis=0)

    def widen_modes(t):
        return jnp.where(same, jnp.concatenate([t] * G, axis=0), 0.0).astype(BF)

    def phase_a(ch):
        blocks(ch, lambda b: [
            (u1, rows(b), (f(q, rows(b)) * f(k, rows(b))).astype(BF))
        ])

    def piece_rows(i):
        return pl.ds(i * (per // PIECES) * L, (per // PIECES) * L)

    def halo(i):
        part_rows = piece_rows(i)
        return remote(
            u1.at[part_rows], u1p.at[part_rows], halo_ss.at[i], halo_rs.at[i],
            seq=lax.rem(me + 1, nseq),
        )

    def halo_back(i):
        part_rows = piece_rows(i)
        return remote(
            dz1.at[part_rows], dz1n.at[part_rows], halo2_ss.at[i], halo2_rs.at[i],
            seq=lax.rem(me + nseq - 1, nseq),
        )

    def x_copy(both, ref, ss, rsem, ch, d, sign):
        to = lax.rem(x + d, X)
        inclusive = jnp.where((to > x) if sign > 0 else (to < x), 1, 0)
        return remote(
            both.at[inclusive, small_rows(ch)], ref.at[x, small_rows(ch)],
            ss.at[ch, d], rsem.at[ch, d], seq=z * X + to,
        )

    def z_copy(ref, ss, rsem, ch, d, sign):
        to = lax.rem(z + sign * d + Z, Z)
        return remote(
            ref.at[z, small_rows(ch)], ref.at[z, small_rows(ch)], ss.at[ch, d], rsem.at[ch, d],
            seq=to * X + x,
        )

    def phase_b(ch):
        def body(b):
            d2 = (f(go, rows(b)) * f(lv, rows(b))).astype(BF)
            r = row(r_s, b)
            powers = jnp.exp(-r * sub_f)
            high = powers.astype(BF)
            low = (powers - high.astype(F32)).astype(BF)
            amp = jnp.where(pick8, jnp.broadcast_to(row(coef_s, b), (G, L)), 0.0)
            amp_high = amp.astype(BF).astype(F32)
            amps = jnp.concatenate([amp_high, amp - amp_high], axis=0).astype(BF)
            h = dot(amps, high, NT) + dot(amps, low, NT)
            state = squeeze_modes(dot(d2, high, NN))
            return [
                (dz2, rows(b), d2),
                (tp, b, high),
                (tq, b, jnp.exp(-r * (L - 1.0 - sub_f)).astype(BF)),
                (h_s, octet(b), h[:G] + h[G:]),
                (z_b, (z, tile(b)), state.astype(BF)),
            ]

        blocks(ch, body)

    def octet(b):
        return pl.ds(pl.multiple_of(b * G, G), G)

    def circulant(line):
        return pltpu.roll(jnp.broadcast_to(line, (L, L)), 0, 1, stride=1, stride_axis=0)

    def phase_h(ch):
        def body(b):
            h = h_s[octet(b), :]
            d2 = dz2[rows(b), :]
            outs, stores = [], []
            for g in range(0, G, 2):
                mats = [
                    jnp.where(lower, circulant(h[g + i : g + i + 1]), 0.0).astype(BF)
                    for i in range(2)
                ]
                stores += [(hs, b * G + g + i, mats[i]) for i in range(2)]
                pair = dot(d2[g * C : (g + 2) * C], jnp.concatenate(mats, axis=0), NT)
                outs += [pair[:C, :L], pair[C:, L:]]
            return stores + [(du2, rows(b), jnp.concatenate(outs, axis=0))]

        blocks(ch, body, 4)

    def phase_t(ch):
        def body(b):
            lines = f_s[octet(b), :]
            stores = []
            for g in range(G):
                circ = circulant(lines[g : g + 1])
                mat = jnp.concatenate(
                    [jnp.where(lower, 0.0, circ), jnp.where(lower, circ, 0.0)], axis=0
                )
                stores.append((tw, b * G + g, mat.astype(BF)))
            return stores

        blocks(ch, body, 4)

    def mid(ch, zref, both, rref, back):
        def body(b):
            acc = jnp.zeros((C, L), F32)
            for src in range(Z):
                gap = (src - z - 1) if back else (z - 1 - src)
                val = zref[src, tile(b), :].astype(F32)
                acc = acc + jnp.where(gap >= 0, weight(8 * back + X + src, b) * val, 0.0)
            whole = zref[z, tile(b), :].astype(F32) + weight(16, b) * acc
            acc = acc.astype(BF)
            return [
                (both, (0, tile(b)), acc),
                (both, (1, tile(b)), whole.astype(BF)),
                (rref, (x, tile(b)), acc),
            ]

        blocks(ch, body)

    def incoming(b, rref, back):
        acc = jnp.zeros((C, L), F32)
        for src in range(X):
            acc = acc + weight(8 * back + src, b) * rref[src, tile(b), :].astype(F32)
        return acc

    def scaled(b, state):
        return widen_modes(weight(18, b) * state)

    def phase_bz(ch):
        def body(b):
            state = incoming(b, row_b, 1)
            full = du2[rows(b), :] + dot(scaled(b, state), tq[b], NT)
            return [
                (b_in, tile(b), state),
                (du2, rows(b), full),
                (dz1, rows(b), (full * f(lk, rows(b)) * f(v, rows(b))).astype(BF)),
            ]

        blocks(ch, body)

    def phase_k(ch):
        def body(b):
            full = du2[rows(b), :]
            return [
                (glk, rows(b), (full * f(y1_s, rows(b))).astype(BF)),
                (gv, rows(b), (full * f(lk, rows(b)) * z1_s[rows(b), :]).astype(BF)),
            ]

        blocks(ch, body)

    def phase_u(ch):
        def body(b):
            wide = jnp.concatenate([u1p[rows(b), :], u1[rows(b), :]], axis=1)
            outs = []
            for g in range(0, G, 2):
                mats = jnp.concatenate([tw[b * G + g], tw[b * G + g + 1]], axis=1)
                pair = dot(wide[g * C : (g + 2) * C], mats, NN)
                outs += [pair[:C, :L], pair[C:, L:]]
            z1 = jnp.concatenate(outs, axis=0)
            y1 = (f(v, rows(b)) * z1).astype(BF)
            second = (y1.astype(F32) * f(lk, rows(b))).astype(BF)
            state = squeeze_modes(dot(second, tq[b], NN))
            return [
                (y1_s, rows(b), y1),
                (z1_s, rows(b), z1),
                (u2, rows(b), second),
                (s_loc, tile(b), state),
                (z_s, (z, tile(b)), state.astype(BF)),
            ]

        blocks(ch, body)

    def fold(mat):
        return pltpu.roll(mat, 1, 1, stride=1, stride_axis=0).sum(axis=0, keepdims=True)

    unfold = ((sub + lane) % L == 0).astype(F32)

    def masked(flip):
        return jnp.concatenate([flip * group_mask[g] for g in range(G)], axis=0)

    def phase_e(ch):
        def body(b):
            flip = dot(rev, dz1[rows(b), :], NT).astype(BF)
            wide = jnp.concatenate([u1p[rows(b), :], u1[rows(b), :]], axis=1)
            energy = dot(masked(flip), wide, NN)
            sums = [
                fold(jnp.where(keep, energy[g * L : (g + 1) * L, L:], energy[g * L : (g + 1) * L, :L]))
                for g in range(G)
            ]
            return [(lag1, octet(b), jnp.concatenate(sums, axis=0))]

        blocks(ch, body, 4)

    def phase_r(ch):
        def pair(i, carry):
            two = [ch * per + 2 * i, ch * per + 2 * i + 1]
            flips = [masked(dot(rev, dz2[rows(b), :], NT).astype(BF)) for b in two]
            zero = jnp.zeros((L, L), BF)
            seconds = [u2[rows(b), :] for b in two]
            diag = jnp.concatenate(
                [
                    jnp.concatenate([seconds[0], zero], axis=1),
                    jnp.concatenate([zero, seconds[1]], axis=1),
                ],
                axis=0,
            )
            energy = dot(jnp.concatenate(flips, axis=1), diag, NN)
            for j, b in enumerate(two):
                sums = [
                    fold(jnp.where(keep, energy[g * L : (g + 1) * L, j * L : (j + 1) * L], 0.0))
                    for g in range(G)
                ]
                lag2[octet(b), :] = jnp.concatenate(sums, axis=0)
            return carry

        lax.fori_loop(0, per // 2, pair, 0, unroll=2)

    def phase_z(ch):
        def body(b):
            second = u2[rows(b), :]
            outs = []
            for g in range(0, G, 2):
                mats = jnp.concatenate([hs[b * G + g], hs[b * G + g + 1]], axis=1)
                pair = dot(second[g * C : (g + 2) * C], mats, NN)
                outs += [pair[:C, :L], pair[C:, L:]]
            return [(z2i, rows(b), jnp.concatenate(outs, axis=0))]

        blocks(ch, body)

    def phase_gf():
        part[...] = dot_exact(lag1[...], unfold, NN).reshape(nb, G, L)

    def phase_gr():
        first = lane[:G] == 0

        def step(i, carry):
            values = []
            for j in range(BATCH):
                b = i * BATCH + j
                lags = lag2[octet(b), :]
                rest = jnp.where(first, 0.0, lags)
                high = rest.astype(BF).astype(F32)
                both = jnp.concatenate([high, rest - high], axis=0).astype(BF)
                inner = dot(both, tq[b], NN)
                inner = weight(17, b) * (inner[:G] + inner[G:]) + lags[:, 0:1]
                inner = jnp.where(pick8, inner, 0.0).sum(axis=0, keepdims=True)
                cross = (s_loc[tile(b), :] * b_in[tile(b), :]).sum(axis=0, keepdims=True)
                values.append(weight(19, b) * (inner + weight(17, b) * cross))
            for j in range(BATCH):
                res[pl.ds(i * BATCH + j, 1), :] = values[j]
            return carry

        lax.fori_loop(0, nb // BATCH, step, 0)

    def phase_sz(ch):
        def body(b):
            state = incoming(b, row_s, 0)
            full = z2i[rows(b), :] + dot(scaled(b, state), tp[b], NT)
            return [(glv, rows(b), (f(go, rows(b)) * full).astype(BF))]

        blocks(ch, body)

    def phase_d(ch):
        def body(b):
            wide = jnp.concatenate([dz1n[rows(b), :], dz1[rows(b), :]], axis=1)
            outs = []
            for g in range(0, G, 2):
                mats = jnp.concatenate(
                    [
                        jnp.concatenate([tw[b * G + g + i, :L], tw[b * G + g + i, L:]], axis=1)
                        for i in range(2)
                    ],
                    axis=0,
                )
                pair = dot(wide[g * C : (g + 2) * C], mats, NT)
                outs += [pair[:C, :L], pair[C:, L:]]
            du1 = jnp.concatenate(outs, axis=0)
            return [
                (gq, rows(b), (du1 * f(k, rows(b))).astype(BF)),
                (gk, rows(b), (du1 * f(q, rows(b))).astype(BF)),
            ]

        blocks(ch, body)

    def start_x(both, ref, ss, rsem, ch, sign):
        for d in range(1, X):
            x_copy(both, ref, ss, rsem, ch, d, sign).start()

    def wait_x(both, ref, ss, rsem, ch, sign):
        for d in range(1, X):
            x_copy(both, ref, ss, rsem, ch, d, sign).wait_recv()

    def z_there(d, sign):
        return (z + d < Z) if sign > 0 else (z - d >= 0)

    def z_from(d, sign):
        return (z - d >= 0) if sign > 0 else (z + d < Z)

    def start_z(ref, ss, rsem, ch, sign):
        for d in range(1, Z):
            @pl.when(z_there(d, sign))
            def _():
                z_copy(ref, ss, rsem, ch, d, sign).start()

    def wait_z(ref, ss, rsem, ch, sign):
        for d in range(1, Z):
            @pl.when(z_from(d, sign))
            def _():
                z_copy(ref, ss, rsem, ch, d, sign).wait_recv()

    results = ((gq, gq_h), (gk, gk_h), (gv, gv_h), (glk, glk_h), (glv, glv_h))

    def save(i, ch):
        src, dst = results[i]
        part_rows = big_rows(ch)
        return pltpu.make_async_copy(src.at[part_rows], dst.at[part_rows], out_sem.at[i, ch])

    every = range(CHUNKS)

    @pl.when(me == 0)
    def _():
        u1p[...] = jnp.zeros_like(u1p)

    @pl.when(me == nseq - 1)
    def _():
        dz1n[...] = jnp.zeros_like(dz1n)

    def peer(d):
        return lax.rem(me + d, nseq)

    def scatter(d):
        return remote(part.at[peer(d)], rs.at[me], rs_ss.at[d], rs_rs.at[d], seq=peer(d))

    def gather(d):
        return remote(total.at[me], total.at[me], ag_ss.at[d], ag_rs.at[d], seq=peer(d))

    def gather_res(d):
        return remote(res_all.at[me], res_all.at[me], ra_ss.at[d], ra_rs.at[d], seq=peer(d))

    swap = remote(dpx.at[0], dpx.at[1], dp_ss, dp_rs, dp=1 - dp)
    swap_res = remote(res, res_dp, rd_ss, rd_rs, dp=1 - dp)
    peers = range(1, nseq)

    def send_halo(*pieces):
        for i in pieces:
            @pl.when(me < nseq - 1)
            def _():
                halo(i).start()

    def send_back(*pieces):
        for i in pieces:
            @pl.when(me > 0)
            def _():
                halo_back(i).start()

    def run_u(ch):
        for i in range(ch * PIECES, (ch + 1) * PIECES):
            @pl.when(me > 0)
            def _():
                halo(i).wait_recv()
        phase_u(ch)
        start_z(z_s, zs_ss, zs_rs, ch, 1)

    def run_bz(ch):
        wait_x(tc_b, row_b, xb_ss, xb_rs, ch, -1)
        phase_bz(ch)

    def run_mid_b(ch):
        wait_z(z_b, zb_ss, zb_rs, ch, -1)
        mid(ch, z_b, tc_b, row_b, 1)
        start_x(tc_b, row_b, xb_ss, xb_rs, ch, -1)

    def run_mid_s(ch):
        wait_z(z_s, zs_ss, zs_rs, ch, 1)
        mid(ch, z_s, tc_s, row_s, 0)
        start_x(tc_s, row_s, xs_ss, xs_rs, ch, 1)

    def run_d(ch):
        for i in range(ch * PIECES, (ch + 1) * PIECES):
            @pl.when(me < nseq - 1)
            def _():
                halo_back(i).wait_recv()
        phase_d(ch)
        save(0, ch).start()
        save(1, ch).start()

    def run_sz(ch):
        wait_x(tc_s, row_s, xs_ss, xs_rs, ch, 1)
        phase_sz(ch)
        save(4, ch).start()

    def run_k(ch):
        phase_k(ch)
        save(2, ch).start()
        save(3, ch).start()

    loads[0].wait()
    loads[1].wait()
    for ch in every:
        phase_a(ch)
    loads[2].wait()
    loads[3].wait()
    sel = (
        lax.broadcasted_iota(jnp.int32, (C, L), 1) % C
        == lax.broadcasted_iota(jnp.int32, (C, L), 0)
    ).astype(F32)
    spread = ((sub % G) == (lane // C))

    def to_rows(mat):
        wide = dot_exact(mat, sel, TN)
        return jnp.where(spread, wide, 0.0).reshape(nb, G, L).sum(axis=1)

    r_rows = to_rows(rate[...])
    gain_rows = jnp.sqrt(one_minus_exp_neg(2.0 * r_rows))
    r_s[...] = r_rows
    gain_s[...] = gain_rows
    coef_rows = to_rows(resid[...]) * gain_rows
    coef_s[...] = coef_rows

    def decay(steps):
        if isinstance(steps, int):
            return jnp.exp(-r_rows * float(L * steps))
        ok = steps >= 0
        return jnp.where(ok, jnp.exp(-r_rows * (L * jnp.maximum(steps, 0)).astype(F32)), 0.0)

    for back in (0, 1):
        for i in range(X):
            ahead = (i > x) if back else (i < x)
            near = (i - x - 1) if back else (x - 1 - i)
            wt[8 * back + i] = decay(jnp.where(ahead, near, near + X))
        for i in range(Z):
            wt[8 * back + X + i] = decay(X * ((i - z - 1) if back else (z - 1 - i)))
    once = jnp.exp(-r_rows)
    wt[16] = decay(X)
    wt[17] = once
    wt[18] = coef_rows * once
    wt[19] = gain_rows

    pl.semaphore_wait(barrier, nseq)
    send_halo(0, 1)
    loads[4].wait()
    loads[5].wait()
    for ch in every:
        phase_b(ch)
        start_z(z_b, zb_ss, zb_rs, ch, -1)
    loads[6].wait()
    f_s[...] = filt[...].astype(F32)
    for ch in every:
        phase_h(ch)
    phase_t(0)
    for ch in every:
        run_mid_b(ch)
    send_halo(2, 3)
    phase_t(1)
    loads[7].wait()
    loads[8].wait()
    run_u(0)
    run_bz(0)
    send_back(0, 1)
    run_bz(1)
    phase_e(0)
    run_mid_s(0)
    phase_r(0)
    run_k(0)
    phase_z(0)
    run_u(1)
    phase_e(1)
    phase_gf()
    for d in peers:
        scatter(d).start()
    send_back(2)
    rs[me] = part[me]
    phase_r(1)
    phase_gr()
    swap_res.start()
    run_mid_s(1)
    send_back(3)
    phase_z(1)
    swap_res.wait_recv()
    res_all[me] = res[...] + res_dp[...]
    for d in peers:
        gather_res(d).start()
    for d in peers:
        scatter(d).wait_recv()
    own = rs[0]
    for i in range(1, nseq):
        own = own + rs[i]
    dpx[0] = own
    swap.start()
    run_d(0)
    swap.wait_recv()
    total[me] = dpx[0] + dpx[1]
    for d in peers:
        gather(d).start()
    run_sz(0)
    run_k(1)
    run_d(1)
    run_sz(1)
    for d in peers:
        gather_res(d).wait_recv()
    res_sum = res_all[0]
    for i in range(1, nseq):
        res_sum = res_sum + res_all[i]
    wide = jnp.broadcast_to(res_sum[:, None, :], (nb, G, L)).reshape(nb * G, L)
    gr_o[...] = dot_exact(sel, jnp.where(spread, wide, 0.0), NT)
    for d in peers:
        gather(d).wait_recv()
    gf_o[...] = total[...].reshape(nb * G, L)

    for i in range(CHUNKS * PIECES):
        @pl.when(me < nseq - 1)
        def _():
            halo(i).wait_send()

        @pl.when(me > 0)
        def _():
            halo_back(i).wait_send()

    for ch in every:
        for d in range(1, X):
            x_copy(tc_b, row_b, xb_ss, xb_rs, ch, d, -1).wait_send()
            x_copy(tc_s, row_s, xs_ss, xs_rs, ch, d, 1).wait_send()
        for d in range(1, Z):
            @pl.when(z_there(d, -1))
            def _():
                z_copy(z_b, zb_ss, zb_rs, ch, d, -1).wait_send()

            @pl.when(z_there(d, 1))
            def _():
                z_copy(z_s, zs_ss, zs_rs, ch, d, 1).wait_send()

        for i in range(5):
            save(i, ch).wait()
    swap.wait_send()
    swap_res.wait_send()
    for d in peers:
        scatter(d).wait_send()
        gather(d).wait_send()
        gather_res(d).wait_send()


def save_kernel(*refs):
    sems = refs[14]
    copies = [pltpu.make_async_copy(refs[i], refs[7 + i], sems.at[i]) for i in range(7)]
    for copy in copies:
        copy.start()
    for copy in copies:
        copy.wait()


def per_device(nseq, q, k, v, lk, lv, go, filt, resid, rate):
    channels = q.shape[1]
    groups = filt.shape[0]
    nb = channels // L
    Z = nseq // X
    big = jax.ShapeDtypeStruct((channels, L), BF)
    hbm = pl.BlockSpec(memory_space=pl.ANY)
    vmem = pl.BlockSpec(memory_space=pltpu.VMEM)
    dma = pltpu.SemaphoreType.DMA
    bigs = [pltpu.VMEM((channels, L), BF)]
    outs = pl.pallas_call(
        functools.partial(kernel, nseq),
        out_shape=[big] * 5
        + [jax.ShapeDtypeStruct((groups, L), F32), jax.ShapeDtypeStruct((C, groups), F32)],
        in_specs=[pl.BlockSpec(memory_space=pltpu.HBM)] * 9,
        out_specs=[hbm] * 5 + [vmem] * 2,
        scratch_shapes=[
            pltpu.VMEM((groups, L), BF),
            pltpu.VMEM((C, groups), F32),
            pltpu.VMEM((C, groups), F32),
        ]
        + bigs * 11
        + bigs * 6
        + [pltpu.VMEM((channels, L), F32)] * 2
        + [pltpu.VMEM((nb, L, L), BF)] * 2
        + [pltpu.VMEM((groups, L, L), BF), pltpu.VMEM((groups, 2 * L, L), BF)]
        + [pltpu.VMEM((groups, L), F32)] * 4
        + [pltpu.VMEM((nb, L), F32)] * 3
        + [pltpu.VMEM((WEIGHTS, nb, L), F32)]
        + [pltpu.VMEM((nb * C, L), F32)] * 2
        + [pltpu.VMEM((2, nb * C, L), BF)] * 2
        + [pltpu.VMEM((X, nb * C, L), BF)] * 2
        + [pltpu.VMEM((Z, nb * C, L), BF)] * 2
        + [pltpu.VMEM((nseq, G, L), F32)] * 2
        + [pltpu.VMEM((2, G, L), F32), pltpu.VMEM((nseq, G, L), F32)]
        + [pltpu.VMEM((channels, L), BF), pltpu.VMEM((channels, L), F32)]
        + [pltpu.VMEM((nb, L), F32)] * 2
        + [pltpu.VMEM((nseq, nb, L), F32)]
        + [dma((9,)), dma((5, CHUNKS))]
        + [dma((CHUNKS * PIECES,))] * 4
        + [dma((CHUNKS, X))] * 2
        + [dma((CHUNKS, Z))] * 2
        + [dma((CHUNKS, X))] * 2
        + [dma((CHUNKS, Z))] * 2
        + [dma((nseq,))] * 2
        + [dma, dma]
        + [dma((nseq,))] * 2
        + [dma, dma]
        + [dma((nseq,))] * 2,
        compiler_params=pltpu.CompilerParams(
            collective_id=0, has_side_effects=True, vmem_limit_bytes=32 * 1024 * 1024
        ),
        name="hyena_bwd",
    )(
        *[
            pltpu.with_memory_space_constraint(a, pltpu.HBM)
            for a in (q[0], k[0], v[0], lk[0], lv[0], go[0], filt, resid.T, rate.T)
        ]
    )
    outs = pl.pallas_call(
        save_kernel,
        out_shape=[jax.ShapeDtypeStruct(o.shape, o.dtype) for o in outs],
        in_specs=[vmem] * 7,
        out_specs=[hbm] * 7,
        scratch_shapes=[dma((7,))],
        compiler_params=pltpu.CompilerParams(vmem_limit_bytes=16 * 1024 * 1024),
        name="hyena_save",
    )(*outs)
    return tuple(o[None] for o in outs[:5]) + (outs[5], outs[6].T)


def solution(mesh):
    wide = P("dp", "chan", "seq")
    small = P("chan", None)
    return jax.shard_map(
        functools.partial(per_device, mesh.shape["seq"]),
        mesh=mesh,
        in_specs=(wide,) * 6 + (small,) * 3,
        out_specs=(wide,) * 5 + (small,) * 2,
        check_vma=False,
    )
```

```python
import functools

import jax
import jax.numpy as jnp
from jax import lax
from jax.experimental import pallas as pl
from jax.experimental.pallas import tpu as pltpu
from jax.sharding import PartitionSpec as P

MESH = pl.DeviceIdType.MESH
NN = (((1,), (0,)), ((), ()))
NT = (((1,), (1,)), ((), ()))
TN = (((0,), (0,)), ((), ()))
EXACT = lax.Precision.HIGHEST
BF = jnp.bfloat16
F32 = jnp.float32

L = 128
C = 16
G = 8
X = 4
CHUNKS = 2
BATCH = 8
PIECES = 2
WEIGHTS = 20


def dot(a, b, dims):
    return lax.dot_general(a, b, dims, preferred_element_type=F32)


def dot_exact(a, b, dims):
    return lax.dot_general(a, b, dims, precision=EXACT, preferred_element_type=F32)


def one_minus_exp_neg(x):
    acc = jnp.full_like(x, 1.0 / 40320.0)
    for divisor in (5040.0, 720.0, 120.0, 24.0, 6.0, 2.0, 1.0):
        acc = 1.0 / divisor - x * acc
    return x * acc


def kernel(
    nseq, q_h, k_h, v_h, lk_h, lv_h, go_h, filt_h, resid_h, rate_h,
    gq_h, gk_h, gv_h, glk_h, glv_h, gf_o, gr_o,
    filt, resid, rate, q, k, v, lk, lv, go, gq, gk, gv, glk, glv,
    u1, u1p, dz2, dz1, dz1n, u2, du2, z2i,
    tp, tq, hs, tw, h_s, f_s, lag1, lag2,
    r_s, coef_s, gain_s, wt, s_loc, b_in, tc_b, tc_s,
    row_b, row_s, z_b, z_s, part, rs, dpx, total, y1_s, z1_s, res, res_dp, res_all,
    in_sem, out_sem, halo_ss, halo_rs, halo2_ss, halo2_rs,
    xb_ss, xb_rs, zb_ss, zb_rs, xs_ss, xs_rs, zs_ss, zs_rs,
    rs_ss, rs_rs, dp_ss, dp_rs, ag_ss, ag_rs, rd_ss, rd_rs, ra_ss, ra_rs,
):
    channels = q.shape[0]
    nb = channels // L
    per = nb // CHUNKS
    Z = nseq // X
    me = lax.axis_index("seq")
    dp = lax.axis_index("dp")
    z = me // X
    x = me - z * X

    ins = (
        (q_h, q), (k_h, k), (rate_h, rate), (resid_h, resid), (go_h, go),
        (lv_h, lv), (filt_h, filt), (lk_h, lk), (v_h, v),
    )
    loads = [pltpu.make_async_copy(s, d, in_sem.at[i]) for i, (s, d) in enumerate(ins)]
    for load in loads:
        load.start()

    barrier = pltpu.get_barrier_semaphore()
    for d in range(1, nseq):
        pl.semaphore_signal(
            barrier, inc=1, device_id={"seq": lax.rem(me + d, nseq)}, device_id_type=MESH
        )
    pl.semaphore_signal(barrier, inc=1, device_id={"dp": 1 - dp}, device_id_type=MESH)

    def remote(src, dst, ss, rsem, **where):
        return pltpu.make_async_remote_copy(
            src_ref=src, dst_ref=dst, send_sem=ss, recv_sem=rsem,
            device_id=where, device_id_type=MESH,
        )

    sub = lax.broadcasted_iota(jnp.int32, (L, L), 0)
    lane = lax.broadcasted_iota(jnp.int32, (L, L), 1)
    sub_f = sub.astype(F32)
    same = (sub // C) == (lane // C)
    lower = lane >= sub
    rev = (sub + lane == L - 1).astype(F32).astype(BF)
    keep = sub + lane <= L - 1
    pick8 = lax.broadcasted_iota(jnp.int32, (G, L), 1) // C == lax.broadcasted_iota(
        jnp.int32, (G, L), 0
    )
    lane_group = lax.broadcasted_iota(jnp.int32, (1, L), 1) // C
    group_mask = [(lane_group == g).astype(F32).astype(BF) for g in range(G)]

    def rows(b):
        return pl.ds(pl.multiple_of(b * L, L), L)

    def tile(b):
        return pl.ds(pl.multiple_of(b * C, C), C)

    def blocks(ch, body, batch=BATCH):
        def step(i, carry):
            stores = []
            for j in range(batch):
                stores += body(ch * per + i * batch + j)
            for ref, idx, value in stores:
                ref[idx] = value
            return carry

        lax.fori_loop(0, per // batch, step, 0)

    def row(ref, b):
        return ref[pl.ds(b, 1), :]

    def weight(i, b):
        return wt[i, pl.ds(b, 1), :]

    def big_rows(ch):
        return pl.ds(ch * per * L, per * L)

    def small_rows(ch):
        return pl.ds(ch * per * C, per * C)

    def f(ref, idx):
        return ref[idx, :].astype(F32)

    def squeeze_modes(full):
        return jnp.where(same, full, 0.0).reshape(G, C, L).sum(axis=0)

    def widen_modes(t):
        return jnp.where(same, jnp.concatenate([t] * G, axis=0), 0.0).astype(BF)

    def phase_a(ch):
        blocks(ch, lambda b: [
            (u1, rows(b), (f(q, rows(b)) * f(k, rows(b))).astype(BF))
        ])

    def piece_rows(i):
        return pl.ds(i * (per // PIECES) * L, (per // PIECES) * L)

    def halo(i):
        part_rows = piece_rows(i)
        return remote(
            u1.at[part_rows], u1p.at[part_rows], halo_ss.at[i], halo_rs.at[i],
            seq=lax.rem(me + 1, nseq),
        )

    def halo_back(i):
        part_rows = piece_rows(i)
        return remote(
            dz1.at[part_rows], dz1n.at[part_rows], halo2_ss.at[i], halo2_rs.at[i],
            seq=lax.rem(me + nseq - 1, nseq),
        )

    def x_copy(both, ref, ss, rsem, ch, d, sign):
        to = lax.rem(x + d, X)
        inclusive = jnp.where((to > x) if sign > 0 else (to < x), 1, 0)
        return remote(
            both.at[inclusive, small_rows(ch)], ref.at[x, small_rows(ch)],
            ss.at[ch, d], rsem.at[ch, d], seq=z * X + to,
        )

    def z_copy(ref, ss, rsem, ch, d, sign):
        to = lax.rem(z + sign * d + Z, Z)
        return remote(
            ref.at[z, small_rows(ch)], ref.at[z, small_rows(ch)], ss.at[ch, d], rsem.at[ch, d],
            seq=to * X + x,
        )

    def phase_b(ch):
        def body(b):
            d2 = (f(go, rows(b)) * f(lv, rows(b))).astype(BF)
            r = row(r_s, b)
            powers = jnp.exp(-r * sub_f)
            high = powers.astype(BF)
            low = (powers - high.astype(F32)).astype(BF)
            amp = jnp.where(pick8, jnp.broadcast_to(row(coef_s, b), (G, L)), 0.0)
            amp_high = amp.astype(BF).astype(F32)
            amps = jnp.concatenate([amp_high, amp - amp_high], axis=0).astype(BF)
            h = dot(amps, high, NT) + dot(amps, low, NT)
            state = squeeze_modes(dot(d2, high, NN))
            return [
                (dz2, rows(b), d2),
                (tp, b, high),
                (tq, b, jnp.exp(-r * (L - 1.0 - sub_f)).astype(BF)),
                (h_s, octet(b), h[:G] + h[G:]),
                (z_b, (z, tile(b)), state.astype(BF)),
            ]

        blocks(ch, body)

    def octet(b):
        return pl.ds(pl.multiple_of(b * G, G), G)

    def circulant(line):
        return pltpu.roll(jnp.broadcast_to(line, (L, L)), 0, 1, stride=1, stride_axis=0)

    def phase_h(ch):
        def body(b):
            h = h_s[octet(b), :]
            d2 = dz2[rows(b), :]
            outs, stores = [], []
            for g in range(0, G, 2):
                mats = [
                    jnp.where(lower, circulant(h[g + i : g + i + 1]), 0.0).astype(BF)
                    for i in range(2)
                ]
                stores += [(hs, b * G + g + i, mats[i]) for i in range(2)]
                pair = dot(d2[g * C : (g + 2) * C], jnp.concatenate(mats, axis=0), NT)
                outs += [pair[:C, :L], pair[C:, L:]]
            return stores + [(du2, rows(b), jnp.concatenate(outs, axis=0))]

        blocks(ch, body, 4)

    def phase_t(ch):
        def body(b):
            lines = f_s[octet(b), :]
            stores = []
            for g in range(G):
                circ = circulant(lines[g : g + 1])
                mat = jnp.concatenate(
                    [jnp.where(lower, 0.0, circ), jnp.where(lower, circ, 0.0)], axis=0
                )
                stores.append((tw, b * G + g, mat.astype(BF)))
            return stores

        blocks(ch, body, 4)

    def mid(ch, zref, both, rref, back):
        def body(b):
            acc = jnp.zeros((C, L), F32)
            for src in range(Z):
                gap = (src - z - 1) if back else (z - 1 - src)
                val = zref[src, tile(b), :].astype(F32)
                acc = acc + jnp.where(gap >= 0, weight(8 * back + X + src, b) * val, 0.0)
            whole = zref[z, tile(b), :].astype(F32) + weight(16, b) * acc
            acc = acc.astype(BF)
            return [
                (both, (0, tile(b)), acc),
                (both, (1, tile(b)), whole.astype(BF)),
                (rref, (x, tile(b)), acc),
            ]

        blocks(ch, body)

    def incoming(b, rref, back):
        acc = jnp.zeros((C, L), F32)
        for src in range(X):
            acc = acc + weight(8 * back + src, b) * rref[src, tile(b), :].astype(F32)
        return acc

    def scaled(b, state):
        return widen_modes(weight(18, b) * state)

    def phase_bz(ch):
        def body(b):
            state = incoming(b, row_b, 1)
            full = du2[rows(b), :] + dot(scaled(b, state), tq[b], NT)
            return [
                (b_in, tile(b), state),
                (du2, rows(b), full),
                (dz1, rows(b), (full * f(lk, rows(b)) * f(v, rows(b))).astype(BF)),
            ]

        blocks(ch, body)

    def phase_k(ch):
        def body(b):
            full = du2[rows(b), :]
            return [
                (glk, rows(b), (full * f(y1_s, rows(b))).astype(BF)),
                (gv, rows(b), (full * f(lk, rows(b)) * z1_s[rows(b), :]).astype(BF)),
            ]

        blocks(ch, body)

    def phase_u(ch):
        def body(b):
            wide = jnp.concatenate([u1p[rows(b), :], u1[rows(b), :]], axis=1)
            outs = []
            for g in range(0, G, 2):
                mats = jnp.concatenate([tw[b * G + g], tw[b * G + g + 1]], axis=1)
                pair = dot(wide[g * C : (g + 2) * C], mats, NN)
                outs += [pair[:C, :L], pair[C:, L:]]
            z1 = jnp.concatenate(outs, axis=0)
            y1 = (f(v, rows(b)) * z1).astype(BF)
            second = (y1.astype(F32) * f(lk, rows(b))).astype(BF)
            state = squeeze_modes(dot(second, tq[b], NN))
            return [
                (y1_s, rows(b), y1),
                (z1_s, rows(b), z1),
                (u2, rows(b), second),
                (s_loc, tile(b), state),
                (z_s, (z, tile(b)), state.astype(BF)),
            ]

        blocks(ch, body)

    def fold(mat):
        return pltpu.roll(mat, 1, 1, stride=1, stride_axis=0).sum(axis=0, keepdims=True)

    unfold = ((sub + lane) % L == 0).astype(F32)

    def masked(flip):
        return jnp.concatenate([flip * group_mask[g] for g in range(G)], axis=0)

    def phase_e(ch):
        def body(b):
            flip = dot(rev, dz1[rows(b), :], NT).astype(BF)
            wide = jnp.concatenate([u1p[rows(b), :], u1[rows(b), :]], axis=1)
            energy = dot(masked(flip), wide, NN)
            sums = [
                fold(jnp.where(keep, energy[g * L : (g + 1) * L, L:], energy[g * L : (g + 1) * L, :L]))
                for g in range(G)
            ]
            return [(lag1, octet(b), jnp.concatenate(sums, axis=0))]

        blocks(ch, body, 4)

    def phase_r(ch):
        def pair(i, carry):
            two = [ch * per + 2 * i, ch * per + 2 * i + 1]
            flips = [masked(dot(rev, dz2[rows(b), :], NT).astype(BF)) for b in two]
            zero = jnp.zeros((L, L), BF)
            seconds = [u2[rows(b), :] for b in two]
            diag = jnp.concatenate(
                [
                    jnp.concatenate([seconds[0], zero], axis=1),
                    jnp.concatenate([zero, seconds[1]], axis=1),
                ],
                axis=0,
            )
            energy = dot(jnp.concatenate(flips, axis=1), diag, NN)
            for j, b in enumerate(two):
                sums = [
                    fold(jnp.where(keep, energy[g * L : (g + 1) * L, j * L : (j + 1) * L], 0.0))
                    for g in range(G)
                ]
                lag2[octet(b), :] = jnp.concatenate(sums, axis=0)
            return carry

        lax.fori_loop(0, per // 2, pair, 0, unroll=2)

    def phase_z(ch):
        def body(b):
            second = u2[rows(b), :]
            outs = []
            for g in range(0, G, 2):
                mats = jnp.concatenate([hs[b * G + g], hs[b * G + g + 1]], axis=1)
                pair = dot(second[g * C : (g + 2) * C], mats, NN)
                outs += [pair[:C, :L], pair[C:, L:]]
            return [(z2i, rows(b), jnp.concatenate(outs, axis=0))]

        blocks(ch, body)

    def phase_gf():
        part[...] = dot_exact(lag1[...], unfold, NN).reshape(nb, G, L)

    def phase_gr():
        first = lane[:G] == 0

        def step(i, carry):
            values = []
            for j in range(BATCH):
                b = i * BATCH + j
                lags = lag2[octet(b), :]
                rest = jnp.where(first, 0.0, lags)
                high = rest.astype(BF).astype(F32)
                both = jnp.concatenate([high, rest - high], axis=0).astype(BF)
                inner = dot(both, tq[b], NN)
                inner = weight(17, b) * (inner[:G] + inner[G:]) + lags[:, 0:1]
                inner = jnp.where(pick8, inner, 0.0).sum(axis=0, keepdims=True)
                cross = (s_loc[tile(b), :] * b_in[tile(b), :]).sum(axis=0, keepdims=True)
                values.append(weight(19, b) * (inner + weight(17, b) * cross))
            for j in range(BATCH):
                res[pl.ds(i * BATCH + j, 1), :] = values[j]
            return carry

        lax.fori_loop(0, nb // BATCH, step, 0)

    def phase_sz(ch):
        def body(b):
            state = incoming(b, row_s, 0)
            full = z2i[rows(b), :] + dot(scaled(b, state), tp[b], NT)
            return [(glv, rows(b), (f(go, rows(b)) * full).astype(BF))]

        blocks(ch, body)

    def phase_d(ch):
        def body(b):
            wide = jnp.concatenate([dz1n[rows(b), :], dz1[rows(b), :]], axis=1)
            outs = []
            for g in range(0, G, 2):
                mats = jnp.concatenate(
                    [
                        jnp.concatenate([tw[b * G + g + i, :L], tw[b * G + g + i, L:]], axis=1)
                        for i in range(2)
                    ],
                    axis=0,
                )
                pair = dot(wide[g * C : (g + 2) * C], mats, NT)
                outs += [pair[:C, :L], pair[C:, L:]]
            du1 = jnp.concatenate(outs, axis=0)
            return [
                (gq, rows(b), (du1 * f(k, rows(b))).astype(BF)),
                (gk, rows(b), (du1 * f(q, rows(b))).astype(BF)),
            ]

        blocks(ch, body)

    def start_x(both, ref, ss, rsem, ch, sign):
        for d in range(1, X):
            x_copy(both, ref, ss, rsem, ch, d, sign).start()

    def wait_x(both, ref, ss, rsem, ch, sign):
        for d in range(1, X):
            x_copy(both, ref, ss, rsem, ch, d, sign).wait_recv()

    def z_there(d, sign):
        return (z + d < Z) if sign > 0 else (z - d >= 0)

    def z_from(d, sign):
        return (z - d >= 0) if sign > 0 else (z + d < Z)

    def start_z(ref, ss, rsem, ch, sign):
        for d in range(1, Z):
            @pl.when(z_there(d, sign))
            def _():
                z_copy(ref, ss, rsem, ch, d, sign).start()

    def wait_z(ref, ss, rsem, ch, sign):
        for d in range(1, Z):
            @pl.when(z_from(d, sign))
            def _():
                z_copy(ref, ss, rsem, ch, d, sign).wait_recv()

    results = ((gq, gq_h), (gk, gk_h), (gv, gv_h), (glk, glk_h), (glv, glv_h))

    def save(i, ch):
        src, dst = results[i]
        part_rows = big_rows(ch)
        return pltpu.make_async_copy(src.at[part_rows], dst.at[part_rows], out_sem.at[i, ch])

    every = range(CHUNKS)

    @pl.when(me == 0)
    def _():
        u1p[...] = jnp.zeros_like(u1p)

    @pl.when(me == nseq - 1)
    def _():
        dz1n[...] = jnp.zeros_like(dz1n)

    def peer(d):
        return lax.rem(me + d, nseq)

    def scatter(d):
        return remote(part.at[peer(d)], rs.at[me], rs_ss.at[d], rs_rs.at[d], seq=peer(d))

    def gather(d):
        return remote(total.at[me], total.at[me], ag_ss.at[d], ag_rs.at[d], seq=peer(d))

    def gather_res(d):
        return remote(res_all.at[me], res_all.at[me], ra_ss.at[d], ra_rs.at[d], seq=peer(d))

    swap = remote(dpx.at[0], dpx.at[1], dp_ss, dp_rs, dp=1 - dp)
    swap_res = remote(res, res_dp, rd_ss, rd_rs, dp=1 - dp)
    peers = range(1, nseq)

    def send_halo(*pieces):
        for i in pieces:
            @pl.when(me < nseq - 1)
            def _():
                halo(i).start()

    def send_back(*pieces):
        for i in pieces:
            @pl.when(me > 0)
            def _():
                halo_back(i).start()

    def run_u(ch):
        for i in range(ch * PIECES, (ch + 1) * PIECES):
            @pl.when(me > 0)
            def _():
                halo(i).wait_recv()
        phase_u(ch)
        start_z(z_s, zs_ss, zs_rs, ch, 1)

    def run_bz(ch):
        wait_x(tc_b, row_b, xb_ss, xb_rs, ch, -1)
        phase_bz(ch)

    def run_mid_b(ch):
        wait_z(z_b, zb_ss, zb_rs, ch, -1)
        mid(ch, z_b, tc_b, row_b, 1)
        start_x(tc_b, row_b, xb_ss, xb_rs, ch, -1)

    def run_mid_s(ch):
        wait_z(z_s, zs_ss, zs_rs, ch, 1)
        mid(ch, z_s, tc_s, row_s, 0)
        start_x(tc_s, row_s, xs_ss, xs_rs, ch, 1)

    def run_d(ch):
        for i in range(ch * PIECES, (ch + 1) * PIECES):
            @pl.when(me < nseq - 1)
            def _():
                halo_back(i).wait_recv()
        phase_d(ch)
        save(0, ch).start()
        save(1, ch).start()

    def run_sz(ch):
        wait_x(tc_s, row_s, xs_ss, xs_rs, ch, 1)
        phase_sz(ch)
        save(4, ch).start()

    def run_k(ch):
        phase_k(ch)
        save(2, ch).start()
        save(3, ch).start()

    loads[0].wait()
    loads[1].wait()
    for ch in every:
        phase_a(ch)
    loads[2].wait()
    loads[3].wait()
    sel = (
        lax.broadcasted_iota(jnp.int32, (C, L), 1) % C
        == lax.broadcasted_iota(jnp.int32, (C, L), 0)
    ).astype(F32)
    spread = ((sub % G) == (lane // C))

    def to_rows(mat):
        wide = dot_exact(mat, sel, TN)
        return jnp.where(spread, wide, 0.0).reshape(nb, G, L).sum(axis=1)

    r_rows = to_rows(rate[...])
    gain_rows = jnp.sqrt(one_minus_exp_neg(2.0 * r_rows))
    r_s[...] = r_rows
    gain_s[...] = gain_rows
    coef_rows = to_rows(resid[...]) * gain_rows
    coef_s[...] = coef_rows

    def decay(steps):
        if isinstance(steps, int):
            return jnp.exp(-r_rows * float(L * steps))
        ok = steps >= 0
        return jnp.where(ok, jnp.exp(-r_rows * (L * jnp.maximum(steps, 0)).astype(F32)), 0.0)

    for back in (0, 1):
        for i in range(X):
            ahead = (i > x) if back else (i < x)
            near = (i - x - 1) if back else (x - 1 - i)
            wt[8 * back + i] = decay(jnp.where(ahead, near, near + X))
        for i in range(Z):
            wt[8 * back + X + i] = decay(X * ((i - z - 1) if back else (z - 1 - i)))
    once = jnp.exp(-r_rows)
    wt[16] = decay(X)
    wt[17] = once
    wt[18] = coef_rows * once
    wt[19] = gain_rows

    pl.semaphore_wait(barrier, nseq)
    send_halo(0, 1)
    loads[4].wait()
    loads[5].wait()
    for ch in every:
        phase_b(ch)
        start_z(z_b, zb_ss, zb_rs, ch, -1)
    loads[6].wait()
    f_s[...] = filt[...].astype(F32)
    for ch in every:
        phase_h(ch)
    phase_t(0)
    for ch in every:
        run_mid_b(ch)
    send_halo(2, 3)
    phase_t(1)
    loads[7].wait()
    loads[8].wait()
    run_u(0)
    run_bz(0)
    send_back(0, 1)
    run_bz(1)
    phase_e(0)
    run_mid_s(0)
    phase_r(0)
    run_k(0)
    phase_z(0)
    send_back(2)
    run_u(1)
    phase_e(1)
    phase_gf()
    for d in peers:
        scatter(d).start()
    rs[me] = part[me]
    phase_r(1)
    phase_gr()
    swap_res.start()
    run_mid_s(1)
    send_back(3)
    phase_z(1)
    swap_res.wait_recv()
    res_all[me] = res[...] + res_dp[...]
    for d in peers:
        gather_res(d).start()
    for d in peers:
        scatter(d).wait_recv()
    own = rs[0]
    for i in range(1, nseq):
        own = own + rs[i]
    dpx[0] = own
    swap.start()
    run_d(0)
    swap.wait_recv()
    total[me] = dpx[0] + dpx[1]
    for d in peers:
        gather(d).start()
    run_sz(0)
    run_k(1)
    run_d(1)
    run_sz(1)
    for d in peers:
        gather_res(d).wait_recv()
    res_sum = res_all[0]
    for i in range(1, nseq):
        res_sum = res_sum + res_all[i]
    wide = jnp.broadcast_to(res_sum[:, None, :], (nb, G, L)).reshape(nb * G, L)
    gr_o[...] = dot_exact(sel, jnp.where(spread, wide, 0.0), NT)
    for d in peers:
        gather(d).wait_recv()
    gf_o[...] = total[...].reshape(nb * G, L)

    for i in range(CHUNKS * PIECES):
        @pl.when(me < nseq - 1)
        def _():
            halo(i).wait_send()

        @pl.when(me > 0)
        def _():
            halo_back(i).wait_send()

    for ch in every:
        for d in range(1, X):
            x_copy(tc_b, row_b, xb_ss, xb_rs, ch, d, -1).wait_send()
            x_copy(tc_s, row_s, xs_ss, xs_rs, ch, d, 1).wait_send()
        for d in range(1, Z):
            @pl.when(z_there(d, -1))
            def _():
                z_copy(z_b, zb_ss, zb_rs, ch, d, -1).wait_send()

            @pl.when(z_there(d, 1))
            def _():
                z_copy(z_s, zs_ss, zs_rs, ch, d, 1).wait_send()

        for i in range(5):
            save(i, ch).wait()
    swap.wait_send()
    swap_res.wait_send()
    for d in peers:
        scatter(d).wait_send()
        gather(d).wait_send()
        gather_res(d).wait_send()


def save_kernel(*refs):
    sems = refs[14]
    copies = [pltpu.make_async_copy(refs[i], refs[7 + i], sems.at[i]) for i in range(7)]
    for copy in copies:
        copy.start()
    for copy in copies:
        copy.wait()


def per_device(nseq, q, k, v, lk, lv, go, filt, resid, rate):
    channels = q.shape[1]
    groups = filt.shape[0]
    nb = channels // L
    Z = nseq // X
    big = jax.ShapeDtypeStruct((channels, L), BF)
    hbm = pl.BlockSpec(memory_space=pl.ANY)
    vmem = pl.BlockSpec(memory_space=pltpu.VMEM)
    dma = pltpu.SemaphoreType.DMA
    bigs = [pltpu.VMEM((channels, L), BF)]
    outs = pl.pallas_call(
        functools.partial(kernel, nseq),
        out_shape=[big] * 5
        + [jax.ShapeDtypeStruct((groups, L), F32), jax.ShapeDtypeStruct((C, groups), F32)],
        in_specs=[pl.BlockSpec(memory_space=pltpu.HBM)] * 9,
        out_specs=[hbm] * 5 + [vmem] * 2,
        scratch_shapes=[
            pltpu.VMEM((groups, L), BF),
            pltpu.VMEM((C, groups), F32),
            pltpu.VMEM((C, groups), F32),
        ]
        + bigs * 11
        + bigs * 6
        + [pltpu.VMEM((channels, L), F32)] * 2
        + [pltpu.VMEM((nb, L, L), BF)] * 2
        + [pltpu.VMEM((groups, L, L), BF), pltpu.VMEM((groups, 2 * L, L), BF)]
        + [pltpu.VMEM((groups, L), F32)] * 4
        + [pltpu.VMEM((nb, L), F32)] * 3
        + [pltpu.VMEM((WEIGHTS, nb, L), F32)]
        + [pltpu.VMEM((nb * C, L), F32)] * 2
        + [pltpu.VMEM((2, nb * C, L), BF)] * 2
        + [pltpu.VMEM((X, nb * C, L), BF)] * 2
        + [pltpu.VMEM((Z, nb * C, L), BF)] * 2
        + [pltpu.VMEM((nseq, G, L), F32)] * 2
        + [pltpu.VMEM((2, G, L), F32), pltpu.VMEM((nseq, G, L), F32)]
        + [pltpu.VMEM((channels, L), BF), pltpu.VMEM((channels, L), F32)]
        + [pltpu.VMEM((nb, L), F32)] * 2
        + [pltpu.VMEM((nseq, nb, L), F32)]
        + [dma((9,)), dma((5, CHUNKS))]
        + [dma((CHUNKS * PIECES,))] * 4
        + [dma((CHUNKS, X))] * 2
        + [dma((CHUNKS, Z))] * 2
        + [dma((CHUNKS, X))] * 2
        + [dma((CHUNKS, Z))] * 2
        + [dma((nseq,))] * 2
        + [dma, dma]
        + [dma((nseq,))] * 2
        + [dma, dma]
        + [dma((nseq,))] * 2,
        compiler_params=pltpu.CompilerParams(
            collective_id=0, has_side_effects=True, vmem_limit_bytes=32 * 1024 * 1024
        ),
        name="hyena_bwd",
    )(
        *[
            pltpu.with_memory_space_constraint(a, pltpu.HBM)
            for a in (q[0], k[0], v[0], lk[0], lv[0], go[0], filt, resid.T, rate.T)
        ]
    )
    outs = pl.pallas_call(
        save_kernel,
        out_shape=[jax.ShapeDtypeStruct(o.shape, o.dtype) for o in outs],
        in_specs=[vmem] * 7,
        out_specs=[hbm] * 7,
        scratch_shapes=[dma((7,))],
        compiler_params=pltpu.CompilerParams(vmem_limit_bytes=16 * 1024 * 1024),
        name="hyena_save",
    )(*outs)
    return tuple(o[None] for o in outs[:5]) + (outs[5], outs[6].T)


def solution(mesh):
    wide = P("dp", "chan", "seq")
    small = P("chan", None)
    return jax.shard_map(
        functools.partial(per_device, mesh.shape["seq"]),
        mesh=mesh,
        in_specs=(wide,) * 6 + (small,) * 3,
        out_specs=(wide,) * 5 + (small,) * 2,
        check_vma=False,
    )
```

```python
import functools

import jax
import jax.numpy as jnp
from jax import lax
from jax.experimental import pallas as pl
from jax.experimental.pallas import tpu as pltpu
from jax.sharding import PartitionSpec as P

MESH = pl.DeviceIdType.MESH
NN = (((1,), (0,)), ((), ()))
NT = (((1,), (1,)), ((), ()))
TN = (((0,), (0,)), ((), ()))
EXACT = lax.Precision.HIGHEST
BF = jnp.bfloat16
F32 = jnp.float32

L = 128
C = 16
G = 8
X = 4
CHUNKS = 2
BATCH = 8
PIECES = 2
WEIGHTS = 20


def dot(a, b, dims):
    return lax.dot_general(a, b, dims, preferred_element_type=F32)


def dot_exact(a, b, dims):
    return lax.dot_general(a, b, dims, precision=EXACT, preferred_element_type=F32)


def one_minus_exp_neg(x):
    acc = jnp.full_like(x, 1.0 / 40320.0)
    for divisor in (5040.0, 720.0, 120.0, 24.0, 6.0, 2.0, 1.0):
        acc = 1.0 / divisor - x * acc
    return x * acc


def kernel(
    nseq, q_h, k_h, v_h, lk_h, lv_h, go_h, filt_h, resid_h, rate_h,
    gq_h, gk_h, gv_h, glk_h, glv_h, gf_o, gr_o,
    filt, resid, rate, q, k, v, lk, lv, go, gq, gk, gv, glk, glv,
    u1, u1p, dz2, dz1, dz1n, u2, du2, z2i,
    tp, tq, hs, tw, h_s, f_s, lag1, lag2,
    r_s, coef_s, gain_s, wt, s_loc, b_in, tc_b, tc_s,
    row_b, row_s, z_b, z_s, part, rs, dpx, total, y1_s, z1_s, res, res_dp, res_all,
    in_sem, out_sem, halo_ss, halo_rs, halo2_ss, halo2_rs,
    xb_ss, xb_rs, zb_ss, zb_rs, xs_ss, xs_rs, zs_ss, zs_rs,
    rs_ss, rs_rs, dp_ss, dp_rs, ag_ss, ag_rs, rd_ss, rd_rs, ra_ss, ra_rs,
):
    channels = q.shape[0]
    nb = channels // L
    per = nb // CHUNKS
    Z = nseq // X
    me = lax.axis_index("seq")
    dp = lax.axis_index("dp")
    z = me // X
    x = me - z * X

    ins = (
        (q_h, q), (k_h, k), (rate_h, rate), (resid_h, resid), (go_h, go),
        (lv_h, lv), (filt_h, filt), (lk_h, lk), (v_h, v),
    )
    loads = [pltpu.make_async_copy(s, d, in_sem.at[i]) for i, (s, d) in enumerate(ins)]
    for load in loads:
        load.start()

    barrier = pltpu.get_barrier_semaphore()
    for d in range(1, nseq):
        pl.semaphore_signal(
            barrier, inc=1, device_id={"seq": lax.rem(me + d, nseq)}, device_id_type=MESH
        )
    pl.semaphore_signal(barrier, inc=1, device_id={"dp": 1 - dp}, device_id_type=MESH)

    def remote(src, dst, ss, rsem, **where):
        return pltpu.make_async_remote_copy(
            src_ref=src, dst_ref=dst, send_sem=ss, recv_sem=rsem,
            device_id=where, device_id_type=MESH,
        )

    sub = lax.broadcasted_iota(jnp.int32, (L, L), 0)
    lane = lax.broadcasted_iota(jnp.int32, (L, L), 1)
    sub_f = sub.astype(F32)
    same = (sub // C) == (lane // C)
    lower = lane >= sub
    rev = (sub + lane == L - 1).astype(F32).astype(BF)
    keep = sub + lane <= L - 1
    pick8 = lax.broadcasted_iota(jnp.int32, (G, L), 1) // C == lax.broadcasted_iota(
        jnp.int32, (G, L), 0
    )
    lane_group = lax.broadcasted_iota(jnp.int32, (1, L), 1) // C
    group_mask = [(lane_group == g).astype(F32).astype(BF) for g in range(G)]

    def rows(b):
        return pl.ds(pl.multiple_of(b * L, L), L)

    def tile(b):
        return pl.ds(pl.multiple_of(b * C, C), C)

    def blocks(ch, body, batch=BATCH):
        def step(i, carry):
            stores = []
            for j in range(batch):
                stores += body(ch * per + i * batch + j)
            for ref, idx, value in stores:
                ref[idx] = value
            return carry

        lax.fori_loop(0, per // batch, step, 0)

    def row(ref, b):
        return ref[pl.ds(b, 1), :]

    def weight(i, b):
        return wt[i, pl.ds(b, 1), :]

    def big_rows(ch):
        return pl.ds(ch * per * L, per * L)

    def small_rows(ch):
        return pl.ds(ch * per * C, per * C)

    def f(ref, idx):
        return ref[idx, :].astype(F32)

    def squeeze_modes(full):
        return jnp.where(same, full, 0.0).reshape(G, C, L).sum(axis=0)

    def widen_modes(t):
        return jnp.where(same, jnp.concatenate([t] * G, axis=0), 0.0).astype(BF)

    def phase_a(ch):
        blocks(ch, lambda b: [
            (u1, rows(b), (f(q, rows(b)) * f(k, rows(b))).astype(BF))
        ])

    def piece_rows(i):
        return pl.ds(i * (per // PIECES) * L, (per // PIECES) * L)

    def halo(i):
        part_rows = piece_rows(i)
        return remote(
            u1.at[part_rows], u1p.at[part_rows], halo_ss.at[i], halo_rs.at[i],
            seq=lax.rem(me + 1, nseq),
        )

    def halo_back(i):
        part_rows = piece_rows(i)
        return remote(
            dz1.at[part_rows], dz1n.at[part_rows], halo2_ss.at[i], halo2_rs.at[i],
            seq=lax.rem(me + nseq - 1, nseq),
        )

    def x_copy(both, ref, ss, rsem, ch, d, sign):
        to = lax.rem(x + d, X)
        inclusive = jnp.where((to > x) if sign > 0 else (to < x), 1, 0)
        return remote(
            both.at[inclusive, small_rows(ch)], ref.at[x, small_rows(ch)],
            ss.at[ch, d], rsem.at[ch, d], seq=z * X + to,
        )

    def z_copy(ref, ss, rsem, ch, d, sign):
        to = lax.rem(z + sign * d + Z, Z)
        return remote(
            ref.at[z, small_rows(ch)], ref.at[z, small_rows(ch)], ss.at[ch, d], rsem.at[ch, d],
            seq=to * X + x,
        )

    def phase_b(ch):
        def body(b):
            d2 = (f(go, rows(b)) * f(lv, rows(b))).astype(BF)
            r = row(r_s, b)
            powers = jnp.exp(-r * sub_f)
            high = powers.astype(BF)
            low = (powers - high.astype(F32)).astype(BF)
            amp = jnp.where(pick8, jnp.broadcast_to(row(coef_s, b), (G, L)), 0.0)
            amp_high = amp.astype(BF).astype(F32)
            amps = jnp.concatenate([amp_high, amp - amp_high], axis=0).astype(BF)
            h = dot(amps, high, NT) + dot(amps, low, NT)
            state = squeeze_modes(dot(d2, high, NN))
            return [
                (dz2, rows(b), d2),
                (tp, b, high),
                (tq, b, jnp.exp(-r * (L - 1.0 - sub_f)).astype(BF)),
                (h_s, octet(b), h[:G] + h[G:]),
                (z_b, (z, tile(b)), state.astype(BF)),
            ]

        blocks(ch, body)

    def octet(b):
        return pl.ds(pl.multiple_of(b * G, G), G)

    def circulant(line):
        return pltpu.roll(jnp.broadcast_to(line, (L, L)), 0, 1, stride=1, stride_axis=0)

    def phase_h(ch):
        def body(b):
            h = h_s[octet(b), :]
            d2 = dz2[rows(b), :]
            outs, stores = [], []
            for g in range(0, G, 2):
                mats = [
                    jnp.where(lower, circulant(h[g + i : g + i + 1]), 0.0).astype(BF)
                    for i in range(2)
                ]
                stores += [(hs, b * G + g + i, mats[i]) for i in range(2)]
                pair = dot(d2[g * C : (g + 2) * C], jnp.concatenate(mats, axis=0), NT)
                outs += [pair[:C, :L], pair[C:, L:]]
            return stores + [(du2, rows(b), jnp.concatenate(outs, axis=0))]

        blocks(ch, body, 4)

    def phase_t(ch):
        def body(b):
            lines = f_s[octet(b), :]
            stores = []
            for g in range(G):
                circ = circulant(lines[g : g + 1])
                mat = jnp.concatenate(
                    [jnp.where(lower, 0.0, circ), jnp.where(lower, circ, 0.0)], axis=0
                )
                stores.append((tw, b * G + g, mat.astype(BF)))
            return stores

        blocks(ch, body, 4)

    def mid(ch, zref, both, rref, back):
        def body(b):
            acc = jnp.zeros((C, L), F32)
            for src in range(Z):
                gap = (src - z - 1) if back else (z - 1 - src)
                val = zref[src, tile(b), :].astype(F32)
                acc = acc + jnp.where(gap >= 0, weight(8 * back + X + src, b) * val, 0.0)
            whole = zref[z, tile(b), :].astype(F32) + weight(16, b) * acc
            acc = acc.astype(BF)
            return [
                (both, (0, tile(b)), acc),
                (both, (1, tile(b)), whole.astype(BF)),
                (rref, (x, tile(b)), acc),
            ]

        blocks(ch, body)

    def incoming(b, rref, back):
        acc = jnp.zeros((C, L), F32)
        for src in range(X):
            acc = acc + weight(8 * back + src, b) * rref[src, tile(b), :].astype(F32)
        return acc

    def scaled(b, state):
        return widen_modes(weight(18, b) * state)

    def phase_bz(ch):
        def body(b):
            state = incoming(b, row_b, 1)
            full = du2[rows(b), :] + dot(scaled(b, state), tq[b], NT)
            return [
                (b_in, tile(b), state),
                (du2, rows(b), full),
                (dz1, rows(b), (full * f(lk, rows(b)) * f(v, rows(b))).astype(BF)),
            ]

        blocks(ch, body)

    def phase_k(ch):
        def body(b):
            full = du2[rows(b), :]
            return [
                (glk, rows(b), (full * f(y1_s, rows(b))).astype(BF)),
                (gv, rows(b), (full * f(lk, rows(b)) * z1_s[rows(b), :]).astype(BF)),
            ]

        blocks(ch, body)

    def phase_u(ch):
        def body(b):
            wide = jnp.concatenate([u1p[rows(b), :], u1[rows(b), :]], axis=1)
            outs = []
            for g in range(0, G, 2):
                mats = jnp.concatenate([tw[b * G + g], tw[b * G + g + 1]], axis=1)
                pair = dot(wide[g * C : (g + 2) * C], mats, NN)
                outs += [pair[:C, :L], pair[C:, L:]]
            z1 = jnp.concatenate(outs, axis=0)
            y1 = (f(v, rows(b)) * z1).astype(BF)
            second = (y1.astype(F32) * f(lk, rows(b))).astype(BF)
            state = squeeze_modes(dot(second, tq[b], NN))
            return [
                (y1_s, rows(b), y1),
                (z1_s, rows(b), z1),
                (u2, rows(b), second),
                (s_loc, tile(b), state),
                (z_s, (z, tile(b)), state.astype(BF)),
            ]

        blocks(ch, body)

    def fold(mat):
        return pltpu.roll(mat, 1, 1, stride=1, stride_axis=0).sum(axis=0, keepdims=True)

    unfold = ((sub + lane) % L == 0).astype(F32)

    def masked(flip):
        return jnp.concatenate([flip * group_mask[g] for g in range(G)], axis=0)

    def phase_e(ch):
        def body(b):
            flip = dot(rev, dz1[rows(b), :], NT).astype(BF)
            wide = jnp.concatenate([u1p[rows(b), :], u1[rows(b), :]], axis=1)
            energy = dot(masked(flip), wide, NN)
            sums = [
                fold(jnp.where(keep, energy[g * L : (g + 1) * L, L:], energy[g * L : (g + 1) * L, :L]))
                for g in range(G)
            ]
            return [(lag1, octet(b), jnp.concatenate(sums, axis=0))]

        blocks(ch, body, 4)

    def phase_r(ch):
        def pair(i, carry):
            two = [ch * per + 2 * i, ch * per + 2 * i + 1]
            flips = [masked(dot(rev, dz2[rows(b), :], NT).astype(BF)) for b in two]
            zero = jnp.zeros((L, L), BF)
            seconds = [u2[rows(b), :] for b in two]
            diag = jnp.concatenate(
                [
                    jnp.concatenate([seconds[0], zero], axis=1),
                    jnp.concatenate([zero, seconds[1]], axis=1),
                ],
                axis=0,
            )
            energy = dot(jnp.concatenate(flips, axis=1), diag, NN)
            for j, b in enumerate(two):
                sums = [
                    fold(jnp.where(keep, energy[g * L : (g + 1) * L, j * L : (j + 1) * L], 0.0))
                    for g in range(G)
                ]
                lag2[octet(b), :] = jnp.concatenate(sums, axis=0)
            return carry

        lax.fori_loop(0, per // 2, pair, 0, unroll=2)

    def phase_z(ch):
        def body(b):
            second = u2[rows(b), :]
            outs = []
            for g in range(0, G, 2):
                mats = jnp.concatenate([hs[b * G + g], hs[b * G + g + 1]], axis=1)
                pair = dot(second[g * C : (g + 2) * C], mats, NN)
                outs += [pair[:C, :L], pair[C:, L:]]
            return [(z2i, rows(b), jnp.concatenate(outs, axis=0))]

        blocks(ch, body)

    def phase_gf():
        part[...] = dot_exact(lag1[...], unfold, NN).reshape(nb, G, L)

    def phase_gr():
        first = lane[:G] == 0

        def step(i, carry):
            values = []
            for j in range(BATCH):
                b = i * BATCH + j
                lags = lag2[octet(b), :]
                rest = jnp.where(first, 0.0, lags)
                high = rest.astype(BF).astype(F32)
                both = jnp.concatenate([high, rest - high], axis=0).astype(BF)
                inner = dot(both, tq[b], NN)
                inner = weight(17, b) * (inner[:G] + inner[G:]) + lags[:, 0:1]
                inner = jnp.where(pick8, inner, 0.0).sum(axis=0, keepdims=True)
                cross = (s_loc[tile(b), :] * b_in[tile(b), :]).sum(axis=0, keepdims=True)
                values.append(weight(19, b) * (inner + weight(17, b) * cross))
            for j in range(BATCH):
                res[pl.ds(i * BATCH + j, 1), :] = values[j]
            return carry

        lax.fori_loop(0, nb // BATCH, step, 0)

    def phase_sz(ch):
        def body(b):
            state = incoming(b, row_s, 0)
            full = z2i[rows(b), :] + dot(scaled(b, state), tp[b], NT)
            return [(glv, rows(b), (f(go, rows(b)) * full).astype(BF))]

        blocks(ch, body)

    def phase_d(ch):
        def body(b):
            wide = jnp.concatenate([dz1n[rows(b), :], dz1[rows(b), :]], axis=1)
            outs = []
            for g in range(0, G, 2):
                mats = jnp.concatenate(
                    [
                        jnp.concatenate([tw[b * G + g + i, :L], tw[b * G + g + i, L:]], axis=1)
                        for i in range(2)
                    ],
                    axis=0,
                )
                pair = dot(wide[g * C : (g + 2) * C], mats, NT)
                outs += [pair[:C, :L], pair[C:, L:]]
            du1 = jnp.concatenate(outs, axis=0)
            return [
                (gq, rows(b), (du1 * f(k, rows(b))).astype(BF)),
                (gk, rows(b), (du1 * f(q, rows(b))).astype(BF)),
            ]

        blocks(ch, body)

    def start_x(both, ref, ss, rsem, ch, sign):
        for d in range(1, X):
            x_copy(both, ref, ss, rsem, ch, d, sign).start()

    def wait_x(both, ref, ss, rsem, ch, sign):
        for d in range(1, X):
            x_copy(both, ref, ss, rsem, ch, d, sign).wait_recv()

    def z_there(d, sign):
        return (z + d < Z) if sign > 0 else (z - d >= 0)

    def z_from(d, sign):
        return (z - d >= 0) if sign > 0 else (z + d < Z)

    def start_z(ref, ss, rsem, ch, sign):
        for d in range(1, Z):
            @pl.when(z_there(d, sign))
            def _():
                z_copy(ref, ss, rsem, ch, d, sign).start()

    def wait_z(ref, ss, rsem, ch, sign):
        for d in range(1, Z):
            @pl.when(z_from(d, sign))
            def _():
                z_copy(ref, ss, rsem, ch, d, sign).wait_recv()

    results = ((gq, gq_h), (gk, gk_h), (gv, gv_h), (glk, glk_h), (glv, glv_h))

    def save(i, ch):
        src, dst = results[i]
        part_rows = big_rows(ch)
        return pltpu.make_async_copy(src.at[part_rows], dst.at[part_rows], out_sem.at[i, ch])

    every = range(CHUNKS)

    @pl.when(me == 0)
    def _():
        u1p[...] = jnp.zeros_like(u1p)

    @pl.when(me == nseq - 1)
    def _():
        dz1n[...] = jnp.zeros_like(dz1n)

    def peer(d):
        return lax.rem(me + d, nseq)

    def scatter(d):
        return remote(part.at[peer(d)], rs.at[me], rs_ss.at[d], rs_rs.at[d], seq=peer(d))

    def gather(d):
        return remote(total.at[me], total.at[me], ag_ss.at[d], ag_rs.at[d], seq=peer(d))

    def gather_res(d):
        return remote(res_all.at[me], res_all.at[me], ra_ss.at[d], ra_rs.at[d], seq=peer(d))

    swap = remote(dpx.at[0], dpx.at[1], dp_ss, dp_rs, dp=1 - dp)
    swap_res = remote(res, res_dp, rd_ss, rd_rs, dp=1 - dp)
    peers = range(1, nseq)

    def send_halo(*pieces):
        for i in pieces:
            @pl.when(me < nseq - 1)
            def _():
                halo(i).start()

    def send_back(*pieces):
        for i in pieces:
            @pl.when(me > 0)
            def _():
                halo_back(i).start()

    def run_u(ch):
        for i in range(ch * PIECES, (ch + 1) * PIECES):
            @pl.when(me > 0)
            def _():
                halo(i).wait_recv()
        phase_u(ch)
        start_z(z_s, zs_ss, zs_rs, ch, 1)

    def run_bz(ch):
        wait_x(tc_b, row_b, xb_ss, xb_rs, ch, -1)
        phase_bz(ch)

    def run_mid_b(ch):
        wait_z(z_b, zb_ss, zb_rs, ch, -1)
        mid(ch, z_b, tc_b, row_b, 1)
        start_x(tc_b, row_b, xb_ss, xb_rs, ch, -1)

    def run_mid_s(ch):
        wait_z(z_s, zs_ss, zs_rs, ch, 1)
        mid(ch, z_s, tc_s, row_s, 0)
        start_x(tc_s, row_s, xs_ss, xs_rs, ch, 1)

    def run_d(ch):
        for i in range(ch * PIECES, (ch + 1) * PIECES):
            @pl.when(me < nseq - 1)
            def _():
                halo_back(i).wait_recv()
        phase_d(ch)
        save(0, ch).start()
        save(1, ch).start()

    def run_sz(ch):
        wait_x(tc_s, row_s, xs_ss, xs_rs, ch, 1)
        phase_sz(ch)
        save(4, ch).start()

    def run_k(ch):
        phase_k(ch)
        save(2, ch).start()
        save(3, ch).start()

    loads[0].wait()
    loads[1].wait()
    for ch in every:
        phase_a(ch)
    loads[2].wait()
    loads[3].wait()
    sel = (
        lax.broadcasted_iota(jnp.int32, (C, L), 1) % C
        == lax.broadcasted_iota(jnp.int32, (C, L), 0)
    ).astype(F32)
    spread = ((sub % G) == (lane // C))

    def to_rows(mat):
        wide = dot_exact(mat, sel, TN)
        return jnp.where(spread, wide, 0.0).reshape(nb, G, L).sum(axis=1)

    r_rows = to_rows(rate[...])
    gain_rows = jnp.sqrt(one_minus_exp_neg(2.0 * r_rows))
    r_s[...] = r_rows
    gain_s[...] = gain_rows
    coef_rows = to_rows(resid[...]) * gain_rows
    coef_s[...] = coef_rows

    def decay(steps):
        if isinstance(steps, int):
            return jnp.exp(-r_rows * float(L * steps))
        ok = steps >= 0
        return jnp.where(ok, jnp.exp(-r_rows * (L * jnp.maximum(steps, 0)).astype(F32)), 0.0)

    for back in (0, 1):
        for i in range(X):
            ahead = (i > x) if back else (i < x)
            near = (i - x - 1) if back else (x - 1 - i)
            wt[8 * back + i] = decay(jnp.where(ahead, near, near + X))
        for i in range(Z):
            wt[8 * back + X + i] = decay(X * ((i - z - 1) if back else (z - 1 - i)))
    once = jnp.exp(-r_rows)
    wt[16] = decay(X)
    wt[17] = once
    wt[18] = coef_rows * once
    wt[19] = gain_rows

    pl.semaphore_wait(barrier, nseq)
    send_halo(0, 1)
    loads[4].wait()
    loads[5].wait()
    for ch in every:
        phase_b(ch)
        start_z(z_b, zb_ss, zb_rs, ch, -1)
    loads[6].wait()
    f_s[...] = filt[...].astype(F32)
    for ch in every:
        phase_h(ch)
    phase_t(0)
    for ch in every:
        run_mid_b(ch)
    send_halo(2, 3)
    phase_t(1)
    loads[7].wait()
    loads[8].wait()
    run_u(0)
    run_bz(0)
    send_back(0, 1)
    run_bz(1)
    phase_e(0)
    run_mid_s(0)
    phase_r(0)
    run_k(0)
    phase_z(0)
    send_back(2)
    run_u(1)
    phase_e(1)
    phase_gf()
    for d in peers:
        scatter(d).start()
    rs[me] = part[me]
    send_back(3)
    phase_r(1)
    phase_gr()
    swap_res.start()
    run_mid_s(1)
    phase_z(1)
    swap_res.wait_recv()
    res_all[me] = res[...] + res_dp[...]
    for d in peers:
        gather_res(d).start()
    for d in peers:
        scatter(d).wait_recv()
    own = rs[0]
    for i in range(1, nseq):
        own = own + rs[i]
    dpx[0] = own
    swap.start()
    run_d(0)
    swap.wait_recv()
    total[me] = dpx[0] + dpx[1]
    for d in peers:
        gather(d).start()
    run_sz(0)
    run_k(1)
    run_d(1)
    run_sz(1)
    for d in peers:
        gather_res(d).wait_recv()
    res_sum = res_all[0]
    for i in range(1, nseq):
        res_sum = res_sum + res_all[i]
    wide = jnp.broadcast_to(res_sum[:, None, :], (nb, G, L)).reshape(nb * G, L)
    gr_o[...] = dot_exact(sel, jnp.where(spread, wide, 0.0), NT)
    for d in peers:
        gather(d).wait_recv()
    gf_o[...] = total[...].reshape(nb * G, L)

    for i in range(CHUNKS * PIECES):
        @pl.when(me < nseq - 1)
        def _():
            halo(i).wait_send()

        @pl.when(me > 0)
        def _():
            halo_back(i).wait_send()

    for ch in every:
        for d in range(1, X):
            x_copy(tc_b, row_b, xb_ss, xb_rs, ch, d, -1).wait_send()
            x_copy(tc_s, row_s, xs_ss, xs_rs, ch, d, 1).wait_send()
        for d in range(1, Z):
            @pl.when(z_there(d, -1))
            def _():
                z_copy(z_b, zb_ss, zb_rs, ch, d, -1).wait_send()

            @pl.when(z_there(d, 1))
            def _():
                z_copy(z_s, zs_ss, zs_rs, ch, d, 1).wait_send()

        for i in range(5):
            save(i, ch).wait()
    swap.wait_send()
    swap_res.wait_send()
    for d in peers:
        scatter(d).wait_send()
        gather(d).wait_send()
        gather_res(d).wait_send()


def save_kernel(*refs):
    sems = refs[14]
    copies = [pltpu.make_async_copy(refs[i], refs[7 + i], sems.at[i]) for i in range(7)]
    for copy in copies:
        copy.start()
    for copy in copies:
        copy.wait()


def per_device(nseq, q, k, v, lk, lv, go, filt, resid, rate):
    channels = q.shape[1]
    groups = filt.shape[0]
    nb = channels // L
    Z = nseq // X
    big = jax.ShapeDtypeStruct((channels, L), BF)
    hbm = pl.BlockSpec(memory_space=pl.ANY)
    vmem = pl.BlockSpec(memory_space=pltpu.VMEM)
    dma = pltpu.SemaphoreType.DMA
    bigs = [pltpu.VMEM((channels, L), BF)]
    outs = pl.pallas_call(
        functools.partial(kernel, nseq),
        out_shape=[big] * 5
        + [jax.ShapeDtypeStruct((groups, L), F32), jax.ShapeDtypeStruct((C, groups), F32)],
        in_specs=[pl.BlockSpec(memory_space=pltpu.HBM)] * 9,
        out_specs=[hbm] * 5 + [vmem] * 2,
        scratch_shapes=[
            pltpu.VMEM((groups, L), BF),
            pltpu.VMEM((C, groups), F32),
            pltpu.VMEM((C, groups), F32),
        ]
        + bigs * 11
        + bigs * 6
        + [pltpu.VMEM((channels, L), F32)] * 2
        + [pltpu.VMEM((nb, L, L), BF)] * 2
        + [pltpu.VMEM((groups, L, L), BF), pltpu.VMEM((groups, 2 * L, L), BF)]
        + [pltpu.VMEM((groups, L), F32)] * 4
        + [pltpu.VMEM((nb, L), F32)] * 3
        + [pltpu.VMEM((WEIGHTS, nb, L), F32)]
        + [pltpu.VMEM((nb * C, L), F32)] * 2
        + [pltpu.VMEM((2, nb * C, L), BF)] * 2
        + [pltpu.VMEM((X, nb * C, L), BF)] * 2
        + [pltpu.VMEM((Z, nb * C, L), BF)] * 2
        + [pltpu.VMEM((nseq, G, L), F32)] * 2
        + [pltpu.VMEM((2, G, L), F32), pltpu.VMEM((nseq, G, L), F32)]
        + [pltpu.VMEM((channels, L), BF), pltpu.VMEM((channels, L), F32)]
        + [pltpu.VMEM((nb, L), F32)] * 2
        + [pltpu.VMEM((nseq, nb, L), F32)]
        + [dma((9,)), dma((5, CHUNKS))]
        + [dma((CHUNKS * PIECES,))] * 4
        + [dma((CHUNKS, X))] * 2
        + [dma((CHUNKS, Z))] * 2
        + [dma((CHUNKS, X))] * 2
        + [dma((CHUNKS, Z))] * 2
        + [dma((nseq,))] * 2
        + [dma, dma]
        + [dma((nseq,))] * 2
        + [dma, dma]
        + [dma((nseq,))] * 2,
        compiler_params=pltpu.CompilerParams(
            collective_id=0, has_side_effects=True, vmem_limit_bytes=32 * 1024 * 1024
        ),
        name="hyena_bwd",
    )(
        *[
            pltpu.with_memory_space_constraint(a, pltpu.HBM)
            for a in (q[0], k[0], v[0], lk[0], lv[0], go[0], filt, resid.T, rate.T)
        ]
    )
    outs = pl.pallas_call(
        save_kernel,
        out_shape=[jax.ShapeDtypeStruct(o.shape, o.dtype) for o in outs],
        in_specs=[vmem] * 7,
        out_specs=[hbm] * 7,
        scratch_shapes=[dma((7,))],
        compiler_params=pltpu.CompilerParams(vmem_limit_bytes=16 * 1024 * 1024),
        name="hyena_save",
    )(*outs)
    return tuple(o[None] for o in outs[:5]) + (outs[5], outs[6].T)


def solution(mesh):
    wide = P("dp", "chan", "seq")
    small = P("chan", None)
    return jax.shard_map(
        functools.partial(per_device, mesh.shape["seq"]),
        mesh=mesh,
        in_specs=(wide,) * 6 + (small,) * 3,
        out_specs=(wide,) * 5 + (small,) * 2,
        check_vma=False,
    )
```
